32 devices in a mesh: group: 2 (over x), gx: 16 (over z, y, core).
Axes of the slice: x: 2, y: 2, z: 4, core: 2. Of those that a mesh axis runs over, the one named last changes fastest.
Arguments:
- out_grad: bfloat16 [1024, 24576], P('group', 'gx'), parts along dimension 0, may hold values from -6 to 6
- pre_act: bfloat16 [1024, 24576], P('group', 'gx'), parts along dimension 0, may hold values from -6 to 6
- layer_input: bfloat16 [1024, 6144], P(('group', 'gx')), parts along dimension 0, may hold values from -0.3984375 to 0.3984375
- weight: bfloat16 [6144, 24576], P(None, 'gx'), may hold values from -0.078125 to 0.078125
Outputs:
- grad_input: bfloat16 [1024, 6144], P(('group', 'gx')), parts along dimension 0
- grad_weight: bfloat16 [6144, 49152], P(None, ('group', 'gx')), parts along dimension 1
The draws below stay inside these ranges and needn't reach their ends.
There are 2 independent parts, one for each index of `group`. The reference program is written for one: setup_inputs(seed, part) draws one part's arguments, and reference() takes and returns one part's arrays. A program takes and returns all parts, laid end to end along the dimension named above; an argument that names none is the same for every part. Nothing has to cross between parts.
All inputs are finite; a program needn't handle non-finite values.
Results may differ from the reference program's by a relative error of at most 0.005.
Values may be sent and summed in bfloat16 or wider, within the bound.
No kernel may reach another device: no remote copies, remote signals or barrier semaphores. Data moves between devices by JAX's collectives and lax.ppermute only.
A program may use at most 192 MiB of HBM per device.

```python
import math
import jax
import jax.numpy as jnp

D = 6144
FF = 24576
TOKENS = 512


def with_spikes(array, stream_key, source, target, parts, factor):
    def block_of(position):
        return (jnp.arange(array.shape[position]) // (array.shape[position] // parts)).reshape((-1,) + (1,) * (array.ndim - 1 - position))

    first = jax.random.permutation(stream_key, parts)[block_of(target)]
    second = (block_of(target) + parts // 2) % parts
    return jnp.where((block_of(source) == first) | (block_of(source) == second), factor * array, array)


def level_of(rng, extent, cuts, low, largest):
    def one(dim, shards_of):
        heights = jax.random.uniform(jax.random.fold_in(jax.random.fold_in(rng, 6), dim), (shards_of,), jnp.float32, low / len(cuts), largest / len(cuts))
        return jnp.repeat(jnp.exp(heights), extent[dim] // shards_of).reshape((-1,) + (1,) * (len(extent) - dim - 1))

    factor_of = one(*cuts[0])
    for cut in cuts[1:]:
        factor_of = factor_of * one(*cut)
    return factor_of


def scatter_about(key, extent, deviation, reach, shards=(), held_as=jnp.bfloat16):
    loudness = level_of(key, extent, shards, -0.22, 0.18) if shards else 1.0
    drawn = jax.random.normal(key, extent, jnp.float32) * deviation * loudness
    return jnp.minimum(jnp.maximum(drawn, -reach), reach).astype(held_as)


def noise_with(stream_key, dims, deviation, limit, pieces, heavy, held_as=jnp.bfloat16):
    array = deviation * jax.random.normal(stream_key, dims, jnp.float32)
    if pieces:
        array = array * level_of(stream_key, dims, pieces, -0.22, 0.18)
    return jnp.clip(with_spikes(array, jax.random.fold_in(stream_key, 3), *heavy), -limit, limit).astype(held_as)


def setup_inputs(seed: int = 0, part: int = 0) -> dict:
    key_list = jax.random.split(jax.random.key(seed), 5)
    part_keys = jax.random.split(jax.random.fold_in(key_list[4], part), 5)
    return {
        "out_grad": noise_with(part_keys[0], (TOKENS, FF), 1.0, 6.0, ((1, 16),), (1, 0, 16, 2.0)),
        "pre_act": scatter_about(part_keys[1], (TOKENS, FF), 1.0, 6.0, ((1, 16),)),
        "layer_input": scatter_about(part_keys[2], (TOKENS, D), 0.06, 0.3984375, ((0, 16),)),
        "weight": scatter_about(key_list[3], (D, FF), D ** -0.5, 0.078125, ((1, 16),)),
    }


def gelu_slope(pre):
    coeff = math.sqrt(2.0 / math.pi)
    inner = coeff * (pre + 0.044715 * pre * pre * pre)
    tanh_value = jnp.tanh(inner)
    return 0.5 * (1.0 + tanh_value) + 0.5 * pre * (1.0 - tanh_value * tanh_value) * coeff * (1.0 + 3.0 * 0.044715 * pre * pre)

def reference(out_grad, pre_act, layer_input, weight):
    slope = gelu_slope(pre_act.astype(jnp.float32))
    grad_hidden = (out_grad.astype(jnp.float32) * slope).astype(jnp.bfloat16)
    grad_input = jnp.dot(grad_hidden, weight.T, preferred_element_type=jnp.float32).astype(jnp.bfloat16)
    grad_weight = jnp.dot(layer_input.T, grad_hidden, preferred_element_type=jnp.float32).astype(jnp.bfloat16)
    return (grad_input, grad_weight)
```

```python
import math

import jax
import jax.numpy as jnp
from jax import lax
from jax.experimental import pallas as pl
from jax.experimental.pallas import tpu as pltpu
from jax.sharding import PartitionSpec as P

CHUNKS = 4
ROWS_BLOCK = 256
VMEM = 48 * 1024 * 1024


def gelu_slope(pre):
    coeff = math.sqrt(2.0 / math.pi)
    inner = coeff * (pre + 0.044715 * pre * pre * pre)
    tanh_value = jnp.tanh(inner)
    return 0.5 * (1.0 + tanh_value) + 0.5 * pre * (1.0 - tanh_value * tanh_value) * coeff * (
        1.0 + 3.0 * 0.044715 * pre * pre
    )


def plain(out_grad, pre_act, layer_input, weight):
    slope = gelu_slope(pre_act.astype(jnp.float32))
    grad_hidden = (out_grad.astype(jnp.float32) * slope).astype(jnp.bfloat16)
    local_grad = lax.dot_general(
        lax.all_gather(layer_input, "gx", axis=0, tiled=True),
        grad_hidden,
        (((0,), (0,)), ((), ())),
        preferred_element_type=jnp.float32,
    )
    grad_input = lax.psum_scatter(
        lax.dot_general(
            grad_hidden, weight, (((1,), (1,)), ((), ())), preferred_element_type=jnp.float32
        ),
        "gx",
        scatter_dimension=0,
        tiled=True,
    ).astype(jnp.bfloat16)
    return (grad_input, local_grad.astype(jnp.bfloat16))


def distance(p):
    return ((p & 3) << 2) | (((p >> 2) & 1) << 1) | (p >> 3)


def hidden_kernel(me_ref, og_ref, pre_ref, dh_ref, *, n, rows):
    me = me_ref[0]
    for p in range(n):
        block = me ^ distance(p)
        at = pl.ds(pl.multiple_of(block * rows, rows), rows)
        pre = pre_ref[at, :].astype(jnp.float32)
        og = og_ref[at, :].astype(jnp.float32)
        dh_ref[pl.ds(p * rows, rows), :] = (og * gelu_slope(pre)).astype(jnp.bfloat16)


def hidden(me, out_grad, pre_act, n):
    tokens, ff = out_grad.shape
    step = 256
    spec = pl.BlockSpec((tokens, step), lambda i, me: (0, i))
    return pl.pallas_call(
        lambda *refs: hidden_kernel(*refs, n=n, rows=tokens // n),
        out_shape=jax.ShapeDtypeStruct((tokens, ff), jnp.bfloat16),
        grid_spec=pltpu.PrefetchScalarGridSpec(
            num_scalar_prefetch=1, grid=(ff // step,), in_specs=[spec, spec], out_specs=spec
        ),
        compiler_params=pltpu.CompilerParams(vmem_limit_bytes=VMEM),
        cost_estimate=pl.CostEstimate(
            flops=tokens * ff * 20, bytes_accessed=tokens * ff * 6, transcendentals=tokens * ff
        ),
        name="hidden",
    )(me, out_grad, pre_act)


def input_kernel(dh_ref, w_ref, keep_ref, send_ref):
    part = lax.dot_general(
        dh_ref[...], w_ref[...], (((1,), (1,)), ((), ())), preferred_element_type=jnp.float32
    ).astype(jnp.bfloat16)
    half = keep_ref.shape[0]
    keep_ref[...] = part[:half]
    send_ref[...] = part[half:]


def input_part(dh, weight, first, count):
    tokens, ff = dh.shape
    out = jax.ShapeDtypeStruct((tokens // 2, count * ROWS_BLOCK), jnp.bfloat16)
    out_spec = pl.BlockSpec((tokens // 2, ROWS_BLOCK), lambda i: (0, i))
    return pl.pallas_call(
        input_kernel,
        out_shape=(out, out),
        grid=(count,),
        in_specs=[
            pl.BlockSpec((tokens, ff), lambda i: (0, 0)),
            pl.BlockSpec((ROWS_BLOCK, ff), lambda i: (first + i, 0)),
        ],
        out_specs=(out_spec, out_spec),
        compiler_params=pltpu.CompilerParams(vmem_limit_bytes=VMEM),
        cost_estimate=pl.CostEstimate(
            flops=2 * tokens * ff * count * ROWS_BLOCK,
            bytes_accessed=2 * (tokens * ff + ff * count * ROWS_BLOCK + tokens * count * ROWS_BLOCK),
            transcendentals=0,
        ),
        name="input_part",
    )(dh, weight)


def weight_kernel(dh_ref, a_ref, b_ref, c_ref, *rest):
    out_ref = rest[-1]
    x = jnp.concatenate([a_ref[...], b_ref[...], c_ref[...]], axis=0)
    out_ref[...] = lax.dot_general(
        x, dh_ref[...], (((0,), (0,)), ((), ())), preferred_element_type=jnp.float32
    ).astype(jnp.bfloat16)


def weight_part(dh, a, b, c, first, total, before):
    tokens, ff = dh.shape
    count = a.shape[1] // ROWS_BLOCK

    def piece(x):
        return pl.BlockSpec((x.shape[0], ROWS_BLOCK), lambda i: (0, i))

    more = () if before is None else (before,)
    return pl.pallas_call(
        weight_kernel,
        out_shape=jax.ShapeDtypeStruct((total, ff), jnp.bfloat16),
        grid=(count,),
        in_specs=[pl.BlockSpec((tokens, ff), lambda i: (0, 0)), piece(a), piece(b), piece(c)]
        + [pl.BlockSpec(memory_space=pl.ANY)] * len(more),
        out_specs=pl.BlockSpec((ROWS_BLOCK, ff), lambda i: (first + i, 0)),
        input_output_aliases={4: 0} if more else {},
        compiler_params=pltpu.CompilerParams(vmem_limit_bytes=VMEM),
        cost_estimate=pl.CostEstimate(
            flops=2 * tokens * ff * count * ROWS_BLOCK,
            bytes_accessed=2 * (tokens * ff + ff * count * ROWS_BLOCK + tokens * count * ROWS_BLOCK),
            transcendentals=0,
        ),
        name="weight_part",
    )(dh, a, b, c, *more)


def add(x, y):
    return (x.astype(jnp.float32) + y.astype(jnp.float32)).astype(jnp.bfloat16)


def after(x, *others):
    return lax.optimization_barrier((x, *others))[0]


def on_device(out_grad, pre_act, layer_input, weight):
    n = lax.axis_size("gx")
    rows, width = layer_input.shape
    if n != 16 or rows % 16:
        return plain(out_grad, pre_act, layer_input, weight)

    def swap(x, bits):
        return lax.ppermute(x, "gx", [(i, i ^ bits) for i in range(n)])

    me = lax.axis_index("gx").astype(jnp.int32).reshape(1)
    wide = width // CHUNKS
    blocks = wide // ROWS_BLOCK

    gathered = []
    last = None
    for j in range(CHUNKS):
        mine = layer_input[:, j * wide : (j + 1) * wide]
        if last is not None:
            mine = after(mine, *last)
        along = [swap(mine, k << 2) for k in (1, 2, 3)]
        last = along
        a = jnp.concatenate([mine] + along, axis=0)
        b = swap(a, 2)
        c = swap(jnp.concatenate([a, b], axis=0), 1)
        gathered.append((a, b, c))

    dh = hidden(me, out_grad, pre_act, n)
    outs = []
    for j in range(CHUNKS):
        keep, send = input_part(dh, weight, j * blocks, blocks)
        part = add(keep, swap(send, 1))
        half = part.shape[0] // 2
        part = add(part[:half], swap(part[half:], 2))
        total = part[:rows].astype(jnp.float32)
        for k in (1, 2, 3):
            total = total + swap(part[k * rows : (k + 1) * rows], k << 2).astype(jnp.float32)
        outs.append(total.astype(jnp.bfloat16))
    grad_input = jnp.concatenate(outs, axis=1)

    grad_weight = None
    for j, (a, b, c) in enumerate(gathered):
        grad_weight = weight_part(dh, a, b, c, j * blocks, width, grad_weight)
    return (grad_input, grad_weight)


def solution(mesh):
    placed = (P("group", "gx"), P("group", "gx"), P(("group", "gx"), None), P(None, "gx"))
    return jax.shard_map(
        on_device,
        mesh=mesh,
        in_specs=placed,
        out_specs=(P(("group", "gx"), None), P(None, ("group", "gx"))),
        check_vma=False,
    )
```

```python
import math

import jax
import jax.numpy as jnp
from jax import lax
from jax.experimental import pallas as pl
from jax.experimental.pallas import tpu as pltpu
from jax.sharding import PartitionSpec as P

RING = 8
PIECES = 4
VMEM_LIMIT = 46 * 1024 * 1024
HIDDEN_LIMIT = 57 * 1024 * 1024
WHOLE = pl.BlockSpec(memory_space=pltpu.VMEM)
OUTSIDE = pl.BlockSpec(memory_space=pltpu.HBM)


def cost(microseconds):
    return pl.CostEstimate(
        flops=int(microseconds * 1.15e9), bytes_accessed=0, transcendentals=0
    )


ANYWHERE = pl.BlockSpec(memory_space=pl.ANY)
SCALAR = pl.BlockSpec(memory_space=pltpu.SMEM)


def gelu_slope(pre):
    coeff = math.sqrt(2.0 / math.pi)
    inner = coeff * (pre + 0.044715 * pre * pre * pre)
    tanh_value = jnp.tanh(inner)
    return 0.5 * (1.0 + tanh_value) + 0.5 * pre * (1.0 - tanh_value * tanh_value) * coeff * (
        1.0 + 3.0 * 0.044715 * pre * pre
    )


def plain(out_grad, pre_act, layer_input, weight):
    slope = gelu_slope(pre_act.astype(jnp.float32))
    grad_hidden = (out_grad.astype(jnp.float32) * slope).astype(jnp.bfloat16)
    local_grad = lax.dot_general(
        lax.all_gather(layer_input, "gx", axis=0, tiled=True),
        grad_hidden,
        (((0,), (0,)), ((), ())),
        preferred_element_type=jnp.float32,
    )
    grad_input = lax.psum_scatter(
        lax.dot_general(
            grad_hidden, weight, (((1,), (1,)), ((), ())), preferred_element_type=jnp.float32
        ),
        "gx",
        scatter_dimension=0,
        tiled=True,
    ).astype(jnp.bfloat16)
    return (grad_input, local_grad.astype(jnp.bfloat16))


def chip_at(place):
    place = place & (RING - 1)
    return jnp.where(place < RING // 2, 2 * place, 2 * (RING - 1 - place) + 1)


def place_of(chip):
    return jnp.where(chip % 2 == 0, chip // 2, RING - 1 - chip // 2)


def ring_pairs():
    path = [2 * p if p < RING // 2 else 2 * (RING - 1 - p) + 1 for p in range(RING)]
    pairs = []
    for place, chip in enumerate(path):
        pairs.append((2 * chip, 2 * path[(place + 1) % RING]))
        pairs.append((2 * chip + 1, 2 * path[(place - 1) % RING] + 1))
    return pairs


def chip_order(me):
    way = jnp.where(me % 2 == 0, 1, -1)
    place = place_of(me // 2)
    steps = [0, -1, -2, -3, 4, 1, 2, 3]
    return [chip_at(place + way * s + RING) for s in steps]


def hidden_kernel(me_ref, og_hbm, pre_hbm, dh_ref, og_ref, pre_ref, sems):
    rows = dh_ref.shape[0] // RING
    copies = []
    for i, chip in enumerate(chip_order(me_ref[0])):
        source = pl.ds(pl.multiple_of(chip * rows, rows), rows)
        block = pl.ds(i * rows, rows)
        pair = (
            pltpu.make_async_copy(og_hbm.at[source, :], og_ref.at[block, :], sems.at[0, i]),
            pltpu.make_async_copy(pre_hbm.at[source, :], pre_ref.at[block, :], sems.at[1, i]),
        )
        for copy in pair:
            copy.start()
        copies.append(pair)
    for i, pair in enumerate(copies):
        for copy in pair:
            copy.wait()
        block = pl.ds(i * rows, rows)
        pre = pre_ref[block, :].astype(jnp.float32)
        og = og_ref[block, :].astype(jnp.float32)
        dh_ref[block, :] = (og * gelu_slope(pre)).astype(jnp.bfloat16)


def hidden(me, out_grad, pre_act):
    shape, dtype = out_grad.shape, out_grad.dtype
    return pl.pallas_call(
        hidden_kernel,
        out_shape=jax.ShapeDtypeStruct(shape, dtype),
        in_specs=[SCALAR, OUTSIDE, OUTSIDE],
        out_specs=WHOLE,
        scratch_shapes=[
            pltpu.VMEM(shape, dtype),
            pltpu.VMEM(shape, dtype),
            pltpu.SemaphoreType.DMA((2, RING)),
        ],
        compiler_params=pltpu.CompilerParams(vmem_limit_bytes=HIDDEN_LIMIT),
        cost_estimate=cost(3),
        name="hidden",
    )(me, out_grad, pre_act)


def prepare_kernel(me_ref, own_ref, twin_ref, mine_ref, other_ref):
    core = me_ref[0] % 2
    rows, half = own_ref.shape[0], mine_ref.shape[1]
    for ref, number in ((mine_ref, core), (other_ref, 1 - core)):
        columns = pl.ds(pl.multiple_of(number * half, half), half)
        ref[pl.ds(pl.multiple_of(core * rows, rows), rows), :] = own_ref[:, columns]
        ref[pl.ds(pl.multiple_of((1 - core) * rows, rows), rows), :] = twin_ref[:, columns]


def prepare(me, own, twin):
    rows, width = own.shape
    out = jax.ShapeDtypeStruct((2 * rows, width // 2), own.dtype)
    return pl.pallas_call(
        prepare_kernel,
        out_shape=(out, out),
        in_specs=[SCALAR, WHOLE, WHOLE],
        out_specs=(WHOLE, WHOLE),
        compiler_params=pltpu.CompilerParams(vmem_limit_bytes=VMEM_LIMIT),
        cost_estimate=cost(1),
        name="prepare",
    )(me, own, twin)


def first_row(me_ref, other, piece, half, wide):
    core = me_ref[0] % 2
    number = 1 - core if other else core
    return pl.multiple_of(number * half + piece * wide, wide)


def input_kernel(me_ref, dh_ref, w_hbm, *refs, other, piece, wide, step):
    outs, (w_ref, part_ref, in_sems, out_sems) = refs[-8:-4], refs[-4:]
    half = outs[0].shape[1]
    row = first_row(me_ref, other, piece, half, wide)
    copies = []
    for i in range(wide // step):
        copy = pltpu.make_async_copy(
            w_hbm.at[pl.ds(pl.multiple_of(row + i * step, step), step), :],
            w_ref.at[pl.ds(i * step, step), :],
            in_sems.at[i],
        )
        copy.start()
        copies.append(copy)
    stores = []
    for i, copy in enumerate(copies):
        copy.wait()
        here = pl.ds(i * step, step)
        part_ref[:, here] = lax.dot_general(
            dh_ref[...], w_ref[here, :], (((1,), (1,)), ((), ())), preferred_element_type=jnp.float32
        ).astype(jnp.bfloat16)
        at = 0
        for j, out in enumerate(outs):
            store = pltpu.make_async_copy(
                part_ref.at[pl.ds(at, out.shape[0]), here],
                out.at[:, pl.ds(piece * wide + i * step, step)],
                out_sems.at[i, j],
            )
            store.start()
            stores.append(store)
            at += out.shape[0]
    for store in stores:
        store.wait()


def input_piece(me, dh, weight, before, other, piece):
    tokens, ff = dh.shape
    half = weight.shape[0] // 2
    wide = half // PIECES
    step = 256
    rows = tokens // RING
    outs = tuple(
        jax.ShapeDtypeStruct((count * rows, half), jnp.bfloat16) for count in (1, 3, 1, 3)
    )
    return pl.pallas_call(
        lambda *refs: input_kernel(*refs, other=other, piece=piece, wide=wide, step=step),
        out_shape=outs,
        in_specs=[SCALAR, WHOLE, OUTSIDE] + [ANYWHERE] * len(before),
        out_specs=(ANYWHERE,) * 4,
        input_output_aliases={3 + i: i for i in range(len(before))},
        scratch_shapes=[
            pltpu.VMEM((wide, ff), jnp.bfloat16),
            pltpu.VMEM((tokens, wide), jnp.bfloat16),
            pltpu.SemaphoreType.DMA((wide // step,)),
            pltpu.SemaphoreType.DMA((wide // step, 4)),
        ],
        compiler_params=pltpu.CompilerParams(vmem_limit_bytes=VMEM_LIMIT),
        cost_estimate=cost(3),
        name="input_piece",
    )(me, dh, weight, *before)


def weight_kernel(me_ref, dh_ref, *refs, other, piece, wide, step):
    blocks, (out_hbm, stage, sems) = refs[:RING], refs[-3:]
    half = blocks[0].shape[1]
    row = first_row(me_ref, other, piece, half, wide)
    x = jnp.concatenate([b[:, pl.ds(piece * wide, wide)] for b in blocks], axis=0)
    copies = []
    for i in range(dh_ref.shape[1] // step):
        columns = pl.ds(i * step, step)
        stage[:, columns] = lax.dot_general(
            x, dh_ref[:, columns], (((0,), (0,)), ((), ())), preferred_element_type=jnp.float32
        ).astype(jnp.bfloat16)
        copy = pltpu.make_async_copy(
            stage.at[:, columns], out_hbm.at[pl.ds(row, wide), columns], sems.at[i]
        )
        copy.start()
        copies.append(copy)
    for copy in copies:
        copy.wait()


def weight_piece(me, dh, blocks, before, other, piece):
    tokens, ff = dh.shape
    half = blocks[0].shape[1]
    wide = half // PIECES
    step = 384
    return pl.pallas_call(
        lambda *refs: weight_kernel(*refs, other=other, piece=piece, wide=wide, step=step),
        out_shape=jax.ShapeDtypeStruct((2 * half, ff), jnp.bfloat16),
        in_specs=[SCALAR, WHOLE] + [WHOLE] * RING + [OUTSIDE] * len(before),
        out_specs=OUTSIDE,
        input_output_aliases={2 + RING: 0} if before else {},
        scratch_shapes=[
            pltpu.VMEM((wide, ff), jnp.bfloat16),
            pltpu.SemaphoreType.DMA((ff // step,)),
        ],
        compiler_params=pltpu.CompilerParams(vmem_limit_bytes=VMEM_LIMIT),
        cost_estimate=cost(3),
        name="weight_piece",
    )(me, dh, *blocks, *before)


def total(*terms):
    result = terms[0].astype(jnp.float32)
    for term in terms[1:]:
        result = result + term.astype(jnp.float32)
    return result.astype(jnp.bfloat16)


def after(x, *others):
    return lax.optimization_barrier((x, *others))[0]


def on_device(out_grad, pre_act, layer_input, weight):
    n = lax.axis_size("gx")
    rows, width = layer_input.shape
    if n != 2 * RING or rows % 16 or width % (2 * PIECES * 256):
        return plain(out_grad, pre_act, layer_input, weight)

    pairs = ring_pairs()
    swaps = [(i, i ^ 1) for i in range(n)]

    def ring(x):
        return lax.ppermute(x, "gx", pairs)

    def swap(x):
        return lax.ppermute(x, "gx", swaps)

    me = lax.axis_index("gx").astype(jnp.int32).reshape(1)
    core = me[0] % 2
    both = 2 * rows

    def block(x, k):
        return x[(k - 1) * both : k * both]

    def product(other, piece, before, *others):
        return input_piece(me, after(dh, *others), weight, before, other, piece)

    m0, o0 = prepare(me, layer_input, swap(layer_input))
    m1 = ring(m0)
    dh = hidden(after(me, m0), out_grad, pre_act)
    o1 = ring(after(o0, dh))
    go = product(True, 0, ())
    m1 = after(m1, go[0])
    m2, sm1 = ring(m1), swap(m1)
    go = product(True, 1, go, m1)
    o1 = after(o1, go[0])
    o2, so1 = ring(o1), swap(o1)
    go = product(True, 2, go, o1)
    m2 = after(m2, go[0])
    m3, sm2 = ring(m2), swap(m2)
    go = product(True, 3, go, m2)
    o2 = after(o2, go[0])
    o3, so2 = ring(o2), swap(o2)
    gm = product(False, 0, (), o2)
    m3 = after(m3, gm[0])
    m4, sm3 = ring(m3), swap(m3)
    own_o, behind_o, opposite_o, ahead_o = go
    from_m, opposite_from = swap(behind_o), swap(opposite_o)
    gm = product(False, 1, gm, m3)
    gm = product(False, 2, gm)
    o3 = after(o3, gm[0])
    so3 = swap(o3)
    gm = product(False, 3, gm, o3, from_m, opposite_from)
    own_m, behind_m, opposite_m, ahead_m = gm
    r4m = ring(total(opposite_m, opposite_from))
    from_o = swap(behind_m)
    m4 = after(m4, gm[0])
    sm4 = swap(m4)
    mine = (m0, m1, m2, m3, m4, so1, so2, so3)
    others = (o0, o1, o2, o3, sm4, sm1, sm2, sm3)

    def gradient(other, piece, before, *ties):
        blocks = others if other else mine
        return weight_piece(me, after(dh, *ties), blocks, before, other, piece)

    def send(ahead, came, k, *ring_terms):
        return ring(total(block(ahead, k), block(came, k), *ring_terms))

    r3o = send(ahead_o, from_o, 3)
    gw = gradient(False, 0, (), from_o)
    r4m = after(r4m, gw)
    r3m = send(ahead_m, from_m, 3, r4m)
    gw = gradient(False, 1, (gw,), r4m)
    r3o = after(r3o, gw)
    r2o = send(ahead_o, from_o, 2, r3o)
    gw = gradient(False, 2, (gw,), r3o)
    r3m = after(r3m, gw)
    r2m = send(ahead_m, from_m, 2, r3m)
    gw = gradient(False, 3, (gw,), r3m)
    r2o = after(r2o, gw)
    r1o = send(ahead_o, from_o, 1, r2o)
    gw = gradient(True, 0, (gw,), r2o)
    r2m = after(r2m, gw)
    r1m = send(ahead_m, from_m, 1, r2m)
    gw = gradient(True, 1, (gw,), r2m)
    gw = gradient(True, 2, (gw,))
    r1o = after(r1o, gw)

    def halves(own, came):
        whole = own.astype(jnp.float32) + came.astype(jnp.float32)
        low, high = whole[:rows], whole[rows:]
        kept = jnp.where(core == 0, low, high)
        return kept, jnp.where(core == 0, high, low).astype(jnp.bfloat16)

    kept_o, sent_o = halves(own_o, r1o)
    came_m = swap(sent_o)
    gw = gradient(True, 3, (gw,), r1o)
    r1m = after(r1m, gw)
    kept_m, sent_m = halves(own_m, r1m)
    came_o = swap(sent_m)
    out_o = (kept_o + came_o.astype(jnp.float32)).astype(jnp.bfloat16)
    out_m = (kept_m + came_m.astype(jnp.float32)).astype(jnp.bfloat16)
    low = jnp.where(core == 0, out_m, out_o)
    high = jnp.where(core == 0, out_o, out_m)
    return (jnp.concatenate([low, high], axis=1), gw)


def solution(mesh):
    placed = (P("group", "gx"), P("group", "gx"), P(("group", "gx"), None), P(None, "gx"))
    return jax.shard_map(
        on_device,
        mesh=mesh,
        in_specs=placed,
        out_specs=(P(("group", "gx"), None), P(None, ("group", "gx"))),
        check_vma=False,
    )
```

```python
import math

import jax
import jax.numpy as jnp
from jax import lax
from jax.experimental import pallas as pl
from jax.experimental.pallas import tpu as pltpu
from jax.sharding import PartitionSpec as P

RING = 8
PIECES = 4
VMEM_LIMIT = 16 * 1024 * 1024
WHOLE = pl.BlockSpec(memory_space=pltpu.VMEM)
OUTSIDE = pl.BlockSpec(memory_space=pltpu.HBM)


def cost(microseconds):
    return pl.CostEstimate(
        flops=int(microseconds * 1.15e9), bytes_accessed=0, transcendentals=0
    )


ANYWHERE = pl.BlockSpec(memory_space=pl.ANY)
SCALAR = pl.BlockSpec(memory_space=pltpu.SMEM)


def gelu_slope(pre):
    coeff = math.sqrt(2.0 / math.pi)
    inner = coeff * (pre + 0.044715 * pre * pre * pre)
    tanh_value = jnp.tanh(inner)
    return 0.5 * (1.0 + tanh_value) + 0.5 * pre * (1.0 - tanh_value * tanh_value) * coeff * (
        1.0 + 3.0 * 0.044715 * pre * pre
    )


def plain(out_grad, pre_act, layer_input, weight):
    slope = gelu_slope(pre_act.astype(jnp.float32))
    grad_hidden = (out_grad.astype(jnp.float32) * slope).astype(jnp.bfloat16)
    local_grad = lax.dot_general(
        lax.all_gather(layer_input, "gx", axis=0, tiled=True),
        grad_hidden,
        (((0,), (0,)), ((), ())),
        preferred_element_type=jnp.float32,
    )
    grad_input = lax.psum_scatter(
        lax.dot_general(
            grad_hidden, weight, (((1,), (1,)), ((), ())), preferred_element_type=jnp.float32
        ),
        "gx",
        scatter_dimension=0,
        tiled=True,
    ).astype(jnp.bfloat16)
    return (grad_input, local_grad.astype(jnp.bfloat16))


def chip_at(place):
    place = place & (RING - 1)
    return jnp.where(place < RING // 2, 2 * place, 2 * (RING - 1 - place) + 1)


def place_of(chip):
    return jnp.where(chip % 2 == 0, chip // 2, RING - 1 - chip // 2)


def ring_pairs():
    path = [2 * p if p < RING // 2 else 2 * (RING - 1 - p) + 1 for p in range(RING)]
    pairs = []
    for place, chip in enumerate(path):
        pairs.append((2 * chip, 2 * path[(place + 1) % RING]))
        pairs.append((2 * chip + 1, 2 * path[(place - 1) % RING] + 1))
    return pairs


def chip_order(me):
    way = jnp.where(me % 2 == 0, 1, -1)
    place = place_of(me // 2)
    steps = [0, -1, -2, -3, 4, 1, 2, 3]
    return [chip_at(place + way * s + RING) for s in steps]


def hidden_kernel(me_ref, og_hbm, pre_hbm, dh_ref, og_ref, pre_ref, sems):
    rows = dh_ref.shape[0] // RING
    copies = []
    for i, chip in enumerate(chip_order(me_ref[0])):
        source = pl.ds(pl.multiple_of(chip * rows, rows), rows)
        block = pl.ds(i * rows, rows)
        pair = (
            pltpu.make_async_copy(og_hbm.at[source, :], og_ref.at[block, :], sems.at[0, i]),
            pltpu.make_async_copy(pre_hbm.at[source, :], pre_ref.at[block, :], sems.at[1, i]),
        )
        for copy in pair:
            copy.start()
        copies.append(pair)
    for i, pair in enumerate(copies):
        for copy in pair:
            copy.wait()
        block = pl.ds(i * rows, rows)
        pre = pre_ref[block, :].astype(jnp.float32)
        og = og_ref[block, :].astype(jnp.float32)
        dh_ref[block, :] = (og * gelu_slope(pre)).astype(jnp.bfloat16)


def hidden(me, out_grad, pre_act):
    shape, dtype = out_grad.shape, out_grad.dtype
    return pl.pallas_call(
        hidden_kernel,
        out_shape=jax.ShapeDtypeStruct(shape, dtype),
        in_specs=[SCALAR, OUTSIDE, OUTSIDE],
        out_specs=WHOLE,
        scratch_shapes=[
            pltpu.VMEM(shape, dtype),
            pltpu.VMEM(shape, dtype),
            pltpu.SemaphoreType.DMA((2, RING)),
        ],
        compiler_params=pltpu.CompilerParams(vmem_limit_bytes=VMEM_LIMIT),
        cost_estimate=cost(3),
        name="hidden",
    )(me, out_grad, pre_act)


def prepare_kernel(me_ref, own_ref, twin_ref, mine_ref, other_ref):
    core = me_ref[0] % 2
    rows, half = own_ref.shape[0], mine_ref.shape[1]
    for ref, number in ((mine_ref, core), (other_ref, 1 - core)):
        columns = pl.ds(pl.multiple_of(number * half, half), half)
        ref[pl.ds(pl.multiple_of(core * rows, rows), rows), :] = own_ref[:, columns]
        ref[pl.ds(pl.multiple_of((1 - core) * rows, rows), rows), :] = twin_ref[:, columns]


def prepare(me, own, twin):
    rows, width = own.shape
    out = jax.ShapeDtypeStruct((2 * rows, width // 2), own.dtype)
    return pl.pallas_call(
        prepare_kernel,
        out_shape=(out, out),
        in_specs=[SCALAR, WHOLE, WHOLE],
        out_specs=(WHOLE, WHOLE),
        compiler_params=pltpu.CompilerParams(vmem_limit_bytes=VMEM_LIMIT),
        cost_estimate=cost(1),
        name="prepare",
    )(me, own, twin)


def first_row(me_ref, other, piece, half, wide):
    core = me_ref[0] % 2
    number = 1 - core if other else core
    return pl.multiple_of(number * half + piece * wide, wide)


def input_kernel(me_ref, dh_ref, w_hbm, *refs, other, piece, wide, step):
    outs, (w_ref, part_ref, in_sems, out_sems) = refs[-8:-4], refs[-4:]
    half = outs[0].shape[1]
    row = first_row(me_ref, other, piece, half, wide)
    copies = []
    for i in range(wide // step):
        copy = pltpu.make_async_copy(
            w_hbm.at[pl.ds(pl.multiple_of(row + i * step, step), step), :],
            w_ref.at[pl.ds(i * step, step), :],
            in_sems.at[i],
        )
        copy.start()
        copies.append(copy)
    stores = []
    for i, copy in enumerate(copies):
        copy.wait()
        here = pl.ds(i * step, step)
        w = w_ref[here, :]
        if other:
            part = lax.dot_general(
                dh_ref[...], w, (((1,), (1,)), ((), ())), preferred_element_type=jnp.float32
            )
        else:
            part = jnp.dot(dh_ref[...], w.T, preferred_element_type=jnp.float32)
        part_ref[:, here] = part.astype(jnp.bfloat16)
        at = 0
        for j, out in enumerate(outs):
            store = pltpu.make_async_copy(
                part_ref.at[pl.ds(at, out.shape[0]), here],
                out.at[:, pl.ds(piece * wide + i * step, step)],
                out_sems.at[i, j],
            )
            store.start()
            stores.append(store)
            at += out.shape[0]
    for store in stores:
        store.wait()


def input_piece(me, dh, weight, before, other, piece):
    tokens, ff = dh.shape
    half = weight.shape[0] // 2
    wide = half // PIECES
    step = 256
    rows = tokens // RING
    outs = tuple(
        jax.ShapeDtypeStruct((count * rows, half), jnp.bfloat16) for count in (1, 3, 1, 3)
    )
    return pl.pallas_call(
        lambda *refs: input_kernel(*refs, other=other, piece=piece, wide=wide, step=step),
        out_shape=outs,
        in_specs=[SCALAR, WHOLE, OUTSIDE] + [ANYWHERE] * len(before),
        out_specs=(ANYWHERE,) * 4,
        input_output_aliases={3 + i: i for i in range(len(before))},
        scratch_shapes=[
            pltpu.VMEM((wide, ff), jnp.bfloat16),
            pltpu.VMEM((tokens, wide), jnp.bfloat16),
            pltpu.SemaphoreType.DMA((wide // step,)),
            pltpu.SemaphoreType.DMA((wide // step, 4)),
        ],
        compiler_params=pltpu.CompilerParams(vmem_limit_bytes=VMEM_LIMIT),
        cost_estimate=cost(3),
        name="input_piece",
    )(me, dh, weight, *before)


def weight_kernel(me_ref, dh_ref, *refs, other, piece, wide, step):
    blocks, (out_hbm, stage, sems) = refs[:RING], refs[-3:]
    half = blocks[0].shape[1]
    row = first_row(me_ref, other, piece, half, wide)
    x = jnp.concatenate([b[:, pl.ds(piece * wide, wide)] for b in blocks], axis=0)
    copies = []
    for i in range(dh_ref.shape[1] // step):
        columns = pl.ds(i * step, step)
        if other:
            result = jnp.dot(x.T, dh_ref[:, columns], preferred_element_type=jnp.float32)
        else:
            result = lax.dot_general(
                x, dh_ref[:, columns], (((0,), (0,)), ((), ())), preferred_element_type=jnp.float32
            )
        stage[:, columns] = result.astype(jnp.bfloat16)
        copy = pltpu.make_async_copy(
            stage.at[:, columns], out_hbm.at[pl.ds(row, wide), columns], sems.at[i]
        )
        copy.start()
        copies.append(copy)
    for copy in copies:
        copy.wait()


def weight_piece(me, dh, blocks, before, other, piece):
    tokens, ff = dh.shape
    half = blocks[0].shape[1]
    wide = half // PIECES
    step = 512 if ff % 512 == 0 else 128
    return pl.pallas_call(
        lambda *refs: weight_kernel(*refs, other=other, piece=piece, wide=wide, step=step),
        out_shape=jax.ShapeDtypeStruct((2 * half, ff), jnp.bfloat16),
        in_specs=[SCALAR, WHOLE] + [WHOLE] * RING + [OUTSIDE] * len(before),
        out_specs=OUTSIDE,
        input_output_aliases={2 + RING: 0} if before else {},
        scratch_shapes=[
            pltpu.VMEM((wide, ff), jnp.bfloat16),
            pltpu.SemaphoreType.DMA((ff // step,)),
        ],
        compiler_params=pltpu.CompilerParams(vmem_limit_bytes=VMEM_LIMIT),
        cost_estimate=cost(3),
        name="weight_piece",
    )(me, dh, *blocks, *before)


def total(*terms):
    result = terms[0].astype(jnp.float32)
    for term in terms[1:]:
        result = result + term.astype(jnp.float32)
    return result.astype(jnp.bfloat16)


def after(x, *others):
    return lax.optimization_barrier((x, *others))[0]


def on_device(out_grad, pre_act, layer_input, weight):
    n = lax.axis_size("gx")
    rows, width = layer_input.shape
    if n != 2 * RING or rows % 16 or width % (2 * PIECES * 256):
        return plain(out_grad, pre_act, layer_input, weight)

    pairs = ring_pairs()
    swaps = [(i, i ^ 1) for i in range(n)]

    def ring(x):
        return lax.ppermute(x, "gx", pairs)

    def swap(x):
        return lax.ppermute(x, "gx", swaps)

    out_grad, pre_act, weight = (
        pltpu.with_memory_space_constraint(x, pltpu.HBM) for x in (out_grad, pre_act, weight)
    )
    me = lax.axis_index("gx").astype(jnp.int32).reshape(1)
    core = me[0] % 2
    both = 2 * rows

    def block(x, k):
        return x[(k - 1) * both : k * both]

    def product(other, piece, before, *others):
        return input_piece(me, after(dh, *others), weight, before, other, piece)

    twin = swap(layer_input)
    dh = hidden(me, out_grad, pre_act)
    m0, o0 = prepare(me, layer_input, after(twin, dh))
    m1 = ring(m0)
    go = product(True, 0, (), m0)
    o1 = ring(after(o0, go[0]))
    m1 = after(m1, go[0])
    m2, sm1 = ring(m1), swap(m1)
    go = product(True, 1, go, m1)
    o1 = after(o1, go[0])
    o2, so1 = ring(o1), swap(o1)
    go = product(True, 2, go, o1)
    m2 = after(m2, go[0])
    m3, sm2 = ring(m2), swap(m2)
    go = product(True, 3, go, m2)
    o2 = after(o2, go[0])
    o3, so2 = ring(o2), swap(o2)
    gm = product(False, 0, (), o2)
    m3 = after(m3, gm[0])
    m4, sm3 = ring(m3), swap(m3)
    own_o, behind_o, opposite_o, ahead_o = go
    from_m, opposite_from = swap(behind_o), swap(opposite_o)
    gm = product(False, 1, gm, m3)
    gm = product(False, 2, gm)
    o3 = after(o3, gm[0])
    so3 = swap(o3)
    gm = product(False, 3, gm, o3, from_m, opposite_from)
    own_m, behind_m, opposite_m, ahead_m = gm
    r4m = ring(total(opposite_m, opposite_from))
    from_o = swap(behind_m)
    m4 = after(m4, gm[0])
    sm4 = swap(m4)
    mine = (m0, m1, m2, m3, m4, so1, so2, so3)
    others = (o0, o1, o2, o3, sm4, sm1, sm2, sm3)

    def gradient(other, piece, before, *ties):
        blocks = others if other else mine
        return weight_piece(me, after(dh, *ties), blocks, before, other, piece)

    def send(ahead, came, k, *ring_terms):
        return ring(total(block(ahead, k), block(came, k), *ring_terms))

    r3o = send(ahead_o, from_o, 3)
    gw = gradient(False, 0, (), from_o)
    r4m = after(r4m, gw)
    r3m = send(ahead_m, from_m, 3, r4m)
    gw = gradient(False, 1, (gw,), r4m)
    r3o = after(r3o, gw)
    r2o = send(ahead_o, from_o, 2, r3o)
    gw = gradient(False, 2, (gw,), r3o)
    r3m = after(r3m, gw)
    r2m = send(ahead_m, from_m, 2, r3m)
    gw = gradient(False, 3, (gw,), r3m)
    r2o = after(r2o, gw)
    r1o = send(ahead_o, from_o, 1, r2o)
    gw = gradient(True, 0, (gw,), r2o)
    r2m = after(r2m, gw)
    r1m = send(ahead_m, from_m, 1, r2m)
    gw = gradient(True, 1, (gw,), r2m)
    gw = gradient(True, 2, (gw,))
    r1o = after(r1o, gw)

    def halves(own, came):
        whole = own.astype(jnp.float32) + came.astype(jnp.float32)
        low, high = whole[:rows], whole[rows:]
        kept = jnp.where(core == 0, low, high)
        return kept, jnp.where(core == 0, high, low).astype(jnp.bfloat16)

    kept_o, sent_o = halves(own_o, r1o)
    came_m = swap(sent_o)
    gw = gradient(True, 3, (gw,), r1o)
    r1m = after(r1m, gw)
    kept_m, sent_m = halves(own_m, r1m)
    came_o = swap(sent_m)
    out_o = (kept_o + came_o.astype(jnp.float32)).astype(jnp.bfloat16)
    out_m = (kept_m + came_m.astype(jnp.float32)).astype(jnp.bfloat16)
    low = jnp.where(core == 0, out_m, out_o)
    high = jnp.where(core == 0, out_o, out_m)
    return (jnp.concatenate([low, high], axis=1), gw)


def solution(mesh):
    placed = (P("group", "gx"), P("group", "gx"), P(("group", "gx"), None), P(None, "gx"))
    return jax.shard_map(
        on_device,
        mesh=mesh,
        in_specs=placed,
        out_specs=(P(("group", "gx"), None), P(None, ("group", "gx"))),
        check_vma=False,
    )
```

```python
import math

import jax
import jax.numpy as jnp
from jax import lax
from jax.experimental import pallas as pl
from jax.experimental.pallas import tpu as pltpu
from jax.sharding import PartitionSpec as P

RING = 8
PIECE_STEPS = 3
PIECES = 4
VMEM_LIMIT = 16 * 1024 * 1024
WHOLE = pl.BlockSpec(memory_space=pltpu.VMEM)
OUTSIDE = pl.BlockSpec(memory_space=pltpu.HBM)


def cost(microseconds):
    return pl.CostEstimate(
        flops=int(microseconds * 1.15e9), bytes_accessed=0, transcendentals=0
    )


ANYWHERE = pl.BlockSpec(memory_space=pl.ANY)
SCALAR = pl.BlockSpec(memory_space=pltpu.SMEM)


def gelu_slope(pre):
    coeff = math.sqrt(2.0 / math.pi)
    inner = coeff * (pre + 0.044715 * pre * pre * pre)
    tanh_value = jnp.tanh(inner)
    return 0.5 * (1.0 + tanh_value) + 0.5 * pre * (1.0 - tanh_value * tanh_value) * coeff * (
        1.0 + 3.0 * 0.044715 * pre * pre
    )


def plain(out_grad, pre_act, layer_input, weight):
    slope = gelu_slope(pre_act.astype(jnp.float32))
    grad_hidden = (out_grad.astype(jnp.float32) * slope).astype(jnp.bfloat16)
    local_grad = lax.dot_general(
        lax.all_gather(layer_input, "gx", axis=0, tiled=True),
        grad_hidden,
        (((0,), (0,)), ((), ())),
        preferred_element_type=jnp.float32,
    )
    grad_input = lax.psum_scatter(
        lax.dot_general(
            grad_hidden, weight, (((1,), (1,)), ((), ())), preferred_element_type=jnp.float32
        ),
        "gx",
        scatter_dimension=0,
        tiled=True,
    ).astype(jnp.bfloat16)
    return (grad_input, local_grad.astype(jnp.bfloat16))


def chip_at(place):
    place = place & (RING - 1)
    return jnp.where(place < RING // 2, 2 * place, 2 * (RING - 1 - place) + 1)


def place_of(chip):
    return jnp.where(chip % 2 == 0, chip // 2, RING - 1 - chip // 2)


def ring_pairs():
    path = [2 * p if p < RING // 2 else 2 * (RING - 1 - p) + 1 for p in range(RING)]
    pairs = []
    for place, chip in enumerate(path):
        pairs.append((2 * chip, 2 * path[(place + 1) % RING]))
        pairs.append((2 * chip + 1, 2 * path[(place - 1) % RING] + 1))
    return pairs


def chip_order(me):
    way = jnp.where(me % 2 == 0, 1, -1)
    place = place_of(me // 2)
    steps = [0, -1, -2, -3, 4, 1, 2, 3]
    return [chip_at(place + way * s + RING) for s in steps]


def hidden_kernel(me_ref, og_hbm, pre_hbm, w_hbm, dh_ref, dht_ref, w_ref, og_ref, pre_ref, sems):
    rows = dh_ref.shape[0] // RING
    copies = []
    for i, chip in enumerate(chip_order(me_ref[0])):
        source = pl.ds(pl.multiple_of(chip * rows, rows), rows)
        block = pl.ds(i * rows, rows)
        pair = (
            pltpu.make_async_copy(og_hbm.at[source, :], og_ref.at[block, :], sems.at[0, i]),
            pltpu.make_async_copy(pre_hbm.at[source, :], pre_ref.at[block, :], sems.at[1, i]),
        )
        for copy in pair:
            copy.start()
        copies.append(pair)
    wide = w_ref.shape[0]
    first = first_row(me_ref, True, 0, w_hbm.shape[0] // 2, wide)
    fetch = pltpu.make_async_copy(w_hbm.at[pl.ds(first, wide), :], w_ref, sems.at[2, 0])
    fetch.start()
    for i, pair in enumerate(copies):
        for copy in pair:
            copy.wait()
        block = pl.ds(i * rows, rows)
        pre = pre_ref[block, :].astype(jnp.float32)
        og = og_ref[block, :].astype(jnp.float32)
        dh_ref[block, :] = (og * gelu_slope(pre)).astype(jnp.bfloat16)
        if i % 2 == 1:
            two = pl.ds((i - 1) * rows, 2 * rows)
            dht_ref[:, two] = dh_ref[two, :].T
    fetch.wait()


def hidden(me, out_grad, pre_act, weight):
    shape, dtype = out_grad.shape, out_grad.dtype
    return pl.pallas_call(
        hidden_kernel,
        out_shape=(
            jax.ShapeDtypeStruct(shape, dtype),
            jax.ShapeDtypeStruct(shape[::-1], dtype),
            jax.ShapeDtypeStruct((weight.shape[0] // (2 * PIECES), shape[1]), dtype),
        ),
        in_specs=[SCALAR, OUTSIDE, OUTSIDE, OUTSIDE],
        out_specs=(WHOLE, WHOLE, WHOLE),
        scratch_shapes=[
            pltpu.VMEM(shape, dtype),
            pltpu.VMEM(shape, dtype),
            pltpu.SemaphoreType.DMA((3, RING)),
        ],
        compiler_params=pltpu.CompilerParams(vmem_limit_bytes=VMEM_LIMIT),
        cost_estimate=cost(1),
        name="hidden",
    )(me, out_grad, pre_act, weight)


def prepare_kernel(me_ref, own_ref, twin_ref, mine_ref, other_ref):
    core = me_ref[0] % 2
    rows, half = own_ref.shape[0], mine_ref.shape[1]
    for ref, number in ((mine_ref, core), (other_ref, 1 - core)):
        columns = pl.ds(pl.multiple_of(number * half, half), half)
        ref[pl.ds(pl.multiple_of(core * rows, rows), rows), :] = own_ref[:, columns]
        ref[pl.ds(pl.multiple_of((1 - core) * rows, rows), rows), :] = twin_ref[:, columns]


def prepare(me, own, twin):
    rows, width = own.shape
    out = jax.ShapeDtypeStruct((2 * rows, width // 2), own.dtype)
    return pl.pallas_call(
        prepare_kernel,
        out_shape=(out, out),
        in_specs=[SCALAR, WHOLE, WHOLE],
        out_specs=(WHOLE, WHOLE),
        compiler_params=pltpu.CompilerParams(vmem_limit_bytes=VMEM_LIMIT),
        cost_estimate=cost(1),
        name="prepare",
    )(me, own, twin)


def first_row(me_ref, other, piece, half, wide):
    core = me_ref[0] % 2
    number = 1 - core if other else core
    return pl.multiple_of(number * half + piece * wide, wide)


def input_kernel(me_ref, dht_ref, w_ref, w_hbm, *refs, other, piece, wide, more):
    outs, part_ref, sems = refs[-7 if more else -6 :][:4], refs[-2], refs[-1]
    half = outs[0].shape[1]
    if more:
        following = (other, piece + 1) if piece + 1 < PIECES else (False, 0)
        fetch = pltpu.make_async_copy(
            w_hbm.at[pl.ds(first_row(me_ref, *following, half, wide), wide), :],
            refs[-3],
            sems.at[PIECE_STEPS, 0],
        )
        fetch.start()
    step = wide // PIECE_STEPS
    stores = []
    for i in range(PIECE_STEPS):
        here = pl.ds(i * step, step)
        part = jnp.dot(w_ref[here, :], dht_ref[...], preferred_element_type=jnp.float32)
        part_ref[:, here] = part.astype(jnp.bfloat16).T
        at = 0
        for j, out in enumerate(outs):
            store = pltpu.make_async_copy(
                part_ref.at[pl.ds(at, out.shape[0]), here],
                out.at[:, pl.ds(piece * wide + i * step, step)],
                sems.at[i, j],
            )
            store.start()
            stores.append(store)
            at += out.shape[0]
    for store in stores:
        store.wait()
    if more:
        fetch.wait()


def input_piece(me, dht, w, weight, before, other, piece):
    ff, tokens = dht.shape
    half = weight.shape[0] // 2
    wide = half // PIECES
    rows = tokens // RING
    more = other or piece + 1 < PIECES
    outs = tuple(
        jax.ShapeDtypeStruct((count * rows, half), jnp.bfloat16) for count in (1, 3, 1, 3)
    )
    following = (jax.ShapeDtypeStruct((wide, ff), jnp.bfloat16),) if more else ()
    result = pl.pallas_call(
        lambda *refs: input_kernel(*refs, other=other, piece=piece, wide=wide, more=more),
        out_shape=outs + following,
        in_specs=[SCALAR, WHOLE, WHOLE, OUTSIDE] + [ANYWHERE] * len(before),
        out_specs=(ANYWHERE,) * 4 + (WHOLE,) * len(following),
        input_output_aliases={4 + i: i for i in range(len(before))},
        scratch_shapes=[
            pltpu.VMEM((tokens, wide), jnp.bfloat16),
            pltpu.SemaphoreType.DMA((PIECE_STEPS + 1, 4)),
        ],
        compiler_params=pltpu.CompilerParams(vmem_limit_bytes=VMEM_LIMIT),
        cost_estimate=cost(1),
        name="input_piece",
    )(me, dht, w, weight, *before)
    return result[:4], (result[4] if more else None)


def weight_kernel(me_ref, dh_ref, *refs, other, piece, wide, step):
    blocks = refs[:RING]
    stage, sems = refs[-2:]
    out_hbm = refs[-3]
    half = blocks[0].shape[1]
    columns = out_hbm.shape[1]
    copies = []
    if piece or other:
        last = (other, piece - 1) if piece else (False, PIECES - 1)
        row = first_row(me_ref, *last, half, wide)
        for i in range(columns // step):
            here = pl.ds(i * step, step)
            copies.append(
                pltpu.make_async_copy(
                    refs[RING].at[:, here], out_hbm.at[pl.ds(row, wide), here], sems.at[0, i]
                )
            )
            copies[-1].start()
    row = first_row(me_ref, other, piece, half, wide)
    x = jnp.concatenate([b[:, pl.ds(piece * wide, wide)] for b in blocks], axis=0).T
    for i in range(columns // step):
        here = pl.ds(i * step, step)
        stage[:, here] = jnp.dot(
            x, dh_ref[:, here], preferred_element_type=jnp.float32
        ).astype(jnp.bfloat16)
        if other and piece == PIECES - 1:
            copies.append(
                pltpu.make_async_copy(
                    stage.at[:, here], out_hbm.at[pl.ds(row, wide), here], sems.at[1, i]
                )
            )
            copies[-1].start()
    for copy in copies:
        copy.wait()


def weight_piece(me, dh, blocks, before, other, piece):
    tokens, ff = dh.shape
    half = blocks[0].shape[1]
    wide = half // PIECES
    step = 512 if ff % 512 == 0 else 128
    return pl.pallas_call(
        lambda *refs: weight_kernel(*refs, other=other, piece=piece, wide=wide, step=step),
        out_shape=(
            jax.ShapeDtypeStruct((2 * half, ff), jnp.bfloat16),
            jax.ShapeDtypeStruct((wide, ff), jnp.bfloat16),
        ),
        in_specs=[SCALAR, WHOLE] + [WHOLE] * RING + ([WHOLE, OUTSIDE] if before else []),
        out_specs=(OUTSIDE, WHOLE),
        input_output_aliases={3 + RING: 0} if before else {},
        scratch_shapes=[pltpu.SemaphoreType.DMA((2, ff // step))],
        compiler_params=pltpu.CompilerParams(vmem_limit_bytes=VMEM_LIMIT),
        cost_estimate=cost(1),
        name="weight_piece",
    )(me, dh, *blocks, *before)


def halves_kernel(me_ref, own_ref, came_ref, kept_ref, sent_ref):
    core = me_ref[0] % 2
    rows = kept_ref.shape[0]
    for ref, number in ((kept_ref, core), (sent_ref, 1 - core)):
        here = pl.ds(pl.multiple_of(number * rows, rows), rows)
        both = own_ref[here, :].astype(jnp.float32) + came_ref[here, :].astype(jnp.float32)
        ref[...] = both.astype(ref.dtype)


def halves(me, own, came):
    shape = (own.shape[0] // 2, own.shape[1])
    return pl.pallas_call(
        halves_kernel,
        out_shape=(
            jax.ShapeDtypeStruct(shape, jnp.float32),
            jax.ShapeDtypeStruct(shape, jnp.bfloat16),
        ),
        in_specs=[SCALAR, WHOLE, WHOLE],
        out_specs=(WHOLE, WHOLE),
        compiler_params=pltpu.CompilerParams(vmem_limit_bytes=VMEM_LIMIT),
        cost_estimate=cost(0.3),
        name="halves",
    )(me, own, came)


def last_kernel(me_ref, mine_ref, mine_came_ref, other_ref, other_came_ref, out_ref):
    core = me_ref[0] % 2
    half = mine_ref.shape[1]
    pairs = ((core, mine_ref, mine_came_ref), (1 - core, other_ref, other_came_ref))
    for number, kept, came in pairs:
        here = pl.ds(pl.multiple_of(number * half, half), half)
        out_ref[:, here] = (kept[...] + came[...].astype(jnp.float32)).astype(out_ref.dtype)


def last(me, mine, mine_came, other, other_came):
    shape = (mine.shape[0], 2 * mine.shape[1])
    return pl.pallas_call(
        last_kernel,
        out_shape=jax.ShapeDtypeStruct(shape, jnp.bfloat16),
        in_specs=[SCALAR] + [WHOLE] * 4,
        out_specs=WHOLE,
        compiler_params=pltpu.CompilerParams(vmem_limit_bytes=VMEM_LIMIT),
        cost_estimate=cost(0.3),
        name="last",
    )(me, mine, mine_came, other, other_came)


def total(*terms):
    result = terms[0].astype(jnp.float32)
    for term in terms[1:]:
        result = result + term.astype(jnp.float32)
    return result.astype(jnp.bfloat16)


def after(x, *others):
    return lax.optimization_barrier((x, *others))[0]


def on_device(out_grad, pre_act, layer_input, weight):
    n = lax.axis_size("gx")
    rows, width = layer_input.shape
    if n != 2 * RING or rows % 16 or width % (2 * PIECES * PIECE_STEPS * 128):
        return plain(out_grad, pre_act, layer_input, weight)

    pairs = ring_pairs()
    swaps = [(i, i ^ 1) for i in range(n)]

    def ring(x):
        return lax.ppermute(x, "gx", pairs)

    def swap(x):
        return lax.ppermute(x, "gx", swaps)

    out_grad, pre_act, weight = (
        pltpu.with_memory_space_constraint(x, pltpu.HBM) for x in (out_grad, pre_act, weight)
    )
    me = lax.axis_index("gx").astype(jnp.int32).reshape(1)
    both = 2 * rows

    def block(x, k):
        return x[(k - 1) * both : k * both]

    def swap_blocks(x):
        return [swap(block(x, k)) for k in (1, 2, 3)]

    twin = swap(layer_input)
    dh, dht, w = hidden(me, out_grad, pre_act, weight)
    m0, o0 = prepare(me, layer_input, after(twin, dh))

    def product(other, piece, w, before, *ties):
        return input_piece(me, after(dht, *ties), w, weight, before, other, piece)

    m1 = ring(m0)
    go, w = product(True, 0, w, (), m0)
    o1 = ring(after(o0, go[0]))
    go, w = product(True, 1, w, go)
    m1 = after(m1, go[0])
    m2, sm1 = ring(m1), swap(m1)
    go, w = product(True, 2, w, go, m1)
    o1 = after(o1, go[0])
    o2, so1 = ring(o1), swap(o1)
    go, w = product(True, 3, w, go, o1)
    m2 = after(m2, go[0])
    m3, sm2 = ring(m2), swap(m2)
    gm, w = product(False, 0, w, (), m2)
    o2 = after(o2, gm[0])
    o3, so2 = ring(o2), swap(o2)
    own_o, behind_o, opposite_o, ahead_o = go
    gm, w = product(False, 1, w, gm, o2, so1)
    m3 = after(m3, gm[0])
    m4, sm3 = ring(m3), swap(m3)
    from_m, opposite_from = swap_blocks(behind_o), swap(opposite_o)
    gm, w = product(False, 2, w, gm, m3, so2)
    o3, m4 = after(o3, gm[0]), after(m4, gm[0])
    so3, sm4 = swap(o3), swap(m4)
    gm, _ = product(False, 3, w, gm, o3, m4, *from_m, opposite_from)
    own_m, behind_m, opposite_m, ahead_m = gm
    r4m = ring(total(opposite_m, opposite_from))
    from_o = swap_blocks(behind_m)
    mine = (m0, m1, m2, m3, m4, so1, so2, so3)
    others = (o0, o1, o2, o3, sm4, sm1, sm2, sm3)

    def gradient(other, piece, before, *ties):
        blocks = others if other else mine
        before = before[::-1]
        return weight_piece(me, after(dh, *ties), blocks, before, other, piece)

    def send(ahead, came, k, *ring_terms):
        return ring(total(block(ahead, k), came[k - 1], *ring_terms))

    r3o = send(ahead_o, from_o, 3)
    gw = gradient(False, 0, (), *from_o)
    r4m = after(r4m, gw[1])
    r3m = send(ahead_m, from_m, 3, r4m)
    gw = gradient(False, 1, gw, r4m)
    r3o = after(r3o, gw[1])
    r2o = send(ahead_o, from_o, 2, r3o)
    gw = gradient(False, 2, gw, r3o)
    r3m = after(r3m, gw[1])
    r2m = send(ahead_m, from_m, 2, r3m)
    gw = gradient(False, 3, gw, r3m)
    r2o = after(r2o, gw[1])
    r1o = send(ahead_o, from_o, 1, r2o)
    gw = gradient(True, 0, gw, r2o)
    r2m = after(r2m, gw[1])
    r1m = send(ahead_m, from_m, 1, r2m)
    gw = gradient(True, 1, gw, r2m)
    gw = gradient(True, 2, gw)
    kept_o, sent_o = halves(me, own_o, after(r1o, gw[1]))
    came_m = swap(sent_o)
    gw = gradient(True, 3, gw, sent_o)
    kept_m, sent_m = halves(me, own_m, after(r1m, gw[1]))
    came_o = swap(sent_m)
    return (last(me, kept_m, came_m, kept_o, came_o), gw[0])


def solution(mesh):
    placed = (P("group", "gx"), P("group", "gx"), P(("group", "gx"), None), P(None, "gx"))
    return jax.shard_map(
        on_device,
        mesh=mesh,
        in_specs=placed,
        out_specs=(P(("group", "gx"), None), P(None, ("group", "gx"))),
        check_vma=False,
    )
```

```python
import math

import jax
import jax.numpy as jnp
from jax import lax
from jax.experimental import pallas as pl
from jax.experimental.pallas import tpu as pltpu
from jax.sharding import PartitionSpec as P

RING = 8
PIECE_STEPS = 3
PIECES = 4
VMEM_LIMIT = 16 * 1024 * 1024
WHOLE = pl.BlockSpec(memory_space=pltpu.VMEM)
OUTSIDE = pl.BlockSpec(memory_space=pltpu.HBM)


def cost(microseconds):
    return pl.CostEstimate(
        flops=int(microseconds * 1.15e9), bytes_accessed=0, transcendentals=0
    )


ANYWHERE = pl.BlockSpec(memory_space=pl.ANY)
SCALAR = pl.BlockSpec(memory_space=pltpu.SMEM)


def gelu_slope(pre):
    coeff = math.sqrt(2.0 / math.pi)
    inner = coeff * (pre + 0.044715 * pre * pre * pre)
    tanh_value = jnp.tanh(inner)
    return 0.5 * (1.0 + tanh_value) + 0.5 * pre * (1.0 - tanh_value * tanh_value) * coeff * (
        1.0 + 3.0 * 0.044715 * pre * pre
    )


def plain(out_grad, pre_act, layer_input, weight):
    slope = gelu_slope(pre_act.astype(jnp.float32))
    grad_hidden = (out_grad.astype(jnp.float32) * slope).astype(jnp.bfloat16)
    local_grad = lax.dot_general(
        lax.all_gather(layer_input, "gx", axis=0, tiled=True),
        grad_hidden,
        (((0,), (0,)), ((), ())),
        preferred_element_type=jnp.float32,
    )
    grad_input = lax.psum_scatter(
        lax.dot_general(
            grad_hidden, weight, (((1,), (1,)), ((), ())), preferred_element_type=jnp.float32
        ),
        "gx",
        scatter_dimension=0,
        tiled=True,
    ).astype(jnp.bfloat16)
    return (grad_input, local_grad.astype(jnp.bfloat16))


def chip_at(place):
    place = place & (RING - 1)
    return jnp.where(place < RING // 2, 2 * place, 2 * (RING - 1 - place) + 1)


def place_of(chip):
    return jnp.where(chip % 2 == 0, chip // 2, RING - 1 - chip // 2)


def ring_pairs():
    path = [2 * p if p < RING // 2 else 2 * (RING - 1 - p) + 1 for p in range(RING)]
    pairs = []
    for place, chip in enumerate(path):
        pairs.append((2 * chip, 2 * path[(place + 1) % RING]))
        pairs.append((2 * chip + 1, 2 * path[(place - 1) % RING] + 1))
    return pairs


def chip_order(me):
    way = jnp.where(me % 2 == 0, 1, -1)
    place = place_of(me // 2)
    steps = [0, -1, -2, -3, 4, 1, 2, 3]
    return [chip_at(place + way * s + RING) for s in steps]


def hidden_kernel(me_ref, og_hbm, pre_hbm, w_hbm, dh_ref, dht_ref, w_ref, og_ref, pre_ref, sems):
    rows = dh_ref.shape[0] // RING
    copies = []
    for i, chip in enumerate(chip_order(me_ref[0])):
        source = pl.ds(pl.multiple_of(chip * rows, rows), rows)
        block = pl.ds(i * rows, rows)
        pair = (
            pltpu.make_async_copy(og_hbm.at[source, :], og_ref.at[block, :], sems.at[0, i]),
            pltpu.make_async_copy(pre_hbm.at[source, :], pre_ref.at[block, :], sems.at[1, i]),
        )
        for copy in pair:
            copy.start()
        copies.append(pair)
    wide = w_ref.shape[0]
    first = first_row(me_ref, True, 0, w_hbm.shape[0] // 2, wide)
    fetch = pltpu.make_async_copy(w_hbm.at[pl.ds(first, wide), :], w_ref, sems.at[2, 0])
    fetch.start()
    for i, pair in enumerate(copies):
        for copy in pair:
            copy.wait()
        block = pl.ds(i * rows, rows)
        pre = pre_ref[block, :].astype(jnp.float32)
        og = og_ref[block, :].astype(jnp.float32)
        dh_ref[block, :] = (og * gelu_slope(pre)).astype(jnp.bfloat16)
        if i % 2 == 1:
            two = pl.ds((i - 1) * rows, 2 * rows)
            dht_ref[:, two] = dh_ref[two, :].T
    fetch.wait()


def hidden(me, out_grad, pre_act, weight):
    shape, dtype = out_grad.shape, out_grad.dtype
    return pl.pallas_call(
        hidden_kernel,
        out_shape=(
            jax.ShapeDtypeStruct(shape, dtype),
            jax.ShapeDtypeStruct(shape[::-1], dtype),
            jax.ShapeDtypeStruct((weight.shape[0] // (2 * PIECES), shape[1]), dtype),
        ),
        in_specs=[SCALAR, OUTSIDE, OUTSIDE, OUTSIDE],
        out_specs=(WHOLE, WHOLE, WHOLE),
        scratch_shapes=[
            pltpu.VMEM(shape, dtype),
            pltpu.VMEM(shape, dtype),
            pltpu.SemaphoreType.DMA((3, RING)),
        ],
        compiler_params=pltpu.CompilerParams(vmem_limit_bytes=VMEM_LIMIT),
        cost_estimate=cost(1),
        name="hidden",
    )(me, out_grad, pre_act, weight)


def prepare_kernel(me_ref, own_ref, twin_ref, mine_ref, other_ref):
    core = me_ref[0] % 2
    rows, half = own_ref.shape[0], mine_ref.shape[1]
    for ref, number in ((mine_ref, core), (other_ref, 1 - core)):
        columns = pl.ds(pl.multiple_of(number * half, half), half)
        ref[pl.ds(pl.multiple_of(core * rows, rows), rows), :] = own_ref[:, columns]
        ref[pl.ds(pl.multiple_of((1 - core) * rows, rows), rows), :] = twin_ref[:, columns]


def fetch_kernel(own_hbm, own_ref, sem):
    copy = pltpu.make_async_copy(own_hbm, own_ref, sem)
    copy.start()
    copy.wait()


def fetch(own):
    return pl.pallas_call(
        fetch_kernel,
        out_shape=jax.ShapeDtypeStruct(own.shape, own.dtype),
        in_specs=[OUTSIDE],
        out_specs=WHOLE,
        scratch_shapes=[pltpu.SemaphoreType.DMA],
        compiler_params=pltpu.CompilerParams(vmem_limit_bytes=VMEM_LIMIT),
        cost_estimate=cost(1),
        name="fetch",
    )(own)


def prepare(me, own, twin):
    rows, width = own.shape
    out = jax.ShapeDtypeStruct((2 * rows, width // 2), own.dtype)
    return pl.pallas_call(
        prepare_kernel,
        out_shape=(out, out),
        in_specs=[SCALAR, WHOLE, WHOLE],
        out_specs=(WHOLE, WHOLE),
        compiler_params=pltpu.CompilerParams(vmem_limit_bytes=VMEM_LIMIT),
        cost_estimate=cost(1),
        name="prepare",
    )(me, own, twin)


def first_row(me_ref, other, piece, half, wide):
    core = me_ref[0] % 2
    number = 1 - core if other else core
    return pl.multiple_of(number * half + piece * wide, wide)


def input_kernel(me_ref, dht_ref, w_ref, w_hbm, *refs, other, piece, wide, more):
    outs, part_ref, sems = refs[-7 if more else -6 :][:4], refs[-2], refs[-1]
    half = outs[0].shape[1]
    if more:
        following = (other, piece + 1) if piece + 1 < PIECES else (False, 0)
        fetch = pltpu.make_async_copy(
            w_hbm.at[pl.ds(first_row(me_ref, *following, half, wide), wide), :],
            refs[-3],
            sems.at[PIECE_STEPS, 0],
        )
        fetch.start()
    steps = PIECE_STEPS if other else 2
    step = wide // steps
    stores = []
    for i in range(steps):
        here = pl.ds(i * step, step)
        part = jnp.dot(w_ref[here, :], dht_ref[...], preferred_element_type=jnp.float32)
        part_ref[:, here] = part.astype(jnp.bfloat16).T
        at = 0
        for j, out in enumerate(outs):
            store = pltpu.make_async_copy(
                part_ref.at[pl.ds(at, out.shape[0]), here],
                out.at[:, pl.ds(piece * wide + i * step, step)],
                sems.at[i, j],
            )
            store.start()
            stores.append(store)
            at += out.shape[0]
    for store in stores:
        store.wait()
    if more:
        fetch.wait()


def input_piece(me, dht, w, weight, before, other, piece):
    ff, tokens = dht.shape
    half = weight.shape[0] // 2
    wide = half // PIECES
    rows = tokens // RING
    more = other or piece + 1 < PIECES
    outs = tuple(
        jax.ShapeDtypeStruct((count * rows, half), jnp.bfloat16) for count in (1, 3, 1, 3)
    )
    following = (jax.ShapeDtypeStruct((wide, ff), jnp.bfloat16),) if more else ()
    result = pl.pallas_call(
        lambda *refs: input_kernel(*refs, other=other, piece=piece, wide=wide, more=more),
        out_shape=outs + following,
        in_specs=[SCALAR, WHOLE, WHOLE, OUTSIDE] + [ANYWHERE] * len(before),
        out_specs=(ANYWHERE,) * 4 + (WHOLE,) * len(following),
        input_output_aliases={4 + i: i for i in range(len(before))},
        scratch_shapes=[
            pltpu.VMEM((tokens, wide), jnp.bfloat16),
            pltpu.SemaphoreType.DMA((PIECE_STEPS + 1, 4)),
        ],
        compiler_params=pltpu.CompilerParams(vmem_limit_bytes=VMEM_LIMIT),
        cost_estimate=cost(1),
        name="input_piece",
    )(me, dht, w, weight, *before)
    return result[:4], (result[4] if more else None)


def weight_kernel(me_ref, dh_ref, *refs, other, piece, wide, step, terms):
    blocks, refs = refs[:RING], refs[RING:]
    if piece or other:
        before_ref, refs = refs[0], refs[2:]
    if terms:
        into = refs[len(terms)]
        total = None
        for ref, k in zip(refs, terms):
            rows = pl.ds(k * into.shape[0], into.shape[0])
            term = ref[rows, :].astype(jnp.float32)
            total = term if total is None else total + term
        into[...] = total.astype(into.dtype)
    out_hbm, stage, sems = refs[-3:]
    half = blocks[0].shape[1]
    columns = out_hbm.shape[1]
    copies = []
    if piece or other:
        last = (other, piece - 1) if piece else (False, PIECES - 1)
        row = first_row(me_ref, *last, half, wide)
        for i in range(columns // step):
            here = pl.ds(i * step, step)
            copies.append(
                pltpu.make_async_copy(
                    before_ref.at[:, here], out_hbm.at[pl.ds(row, wide), here], sems.at[0, i]
                )
            )
            copies[-1].start()
    row = first_row(me_ref, other, piece, half, wide)
    x = jnp.concatenate([b[:, pl.ds(piece * wide, wide)] for b in blocks], axis=0).T
    for i in range(columns // step):
        here = pl.ds(i * step, step)
        stage[:, here] = jnp.dot(
            x, dh_ref[:, here], preferred_element_type=jnp.float32
        ).astype(jnp.bfloat16)
        if other and piece == PIECES - 1:
            copies.append(
                pltpu.make_async_copy(
                    stage.at[:, here], out_hbm.at[pl.ds(row, wide), here], sems.at[1, i]
                )
            )
            copies[-1].start()
    for copy in copies:
        copy.wait()


def weight_piece(me, dh, blocks, before, other, piece, terms=()):
    tokens, ff = dh.shape
    rows, half = blocks[0].shape
    wide = half // PIECES
    step = 512 if ff % 512 == 0 else 128
    sums = (jax.ShapeDtypeStruct((rows, half), jnp.bfloat16),) if terms else ()
    result = pl.pallas_call(
        lambda *refs: weight_kernel(
            *refs, other=other, piece=piece, wide=wide, step=step, terms=[k for _, k in terms]
        ),
        out_shape=sums
        + (
            jax.ShapeDtypeStruct((2 * half, ff), jnp.bfloat16),
            jax.ShapeDtypeStruct((wide, ff), jnp.bfloat16),
        ),
        in_specs=[SCALAR, WHOLE]
        + [WHOLE] * RING
        + ([WHOLE, OUTSIDE] if before else [])
        + [WHOLE] * len(terms),
        out_specs=(WHOLE,) * len(sums) + (OUTSIDE, WHOLE),
        input_output_aliases={3 + RING: len(sums)} if before else {},
        scratch_shapes=[pltpu.SemaphoreType.DMA((2, ff // step))],
        compiler_params=pltpu.CompilerParams(vmem_limit_bytes=VMEM_LIMIT),
        cost_estimate=cost(1),
        name="weight_piece",
    )(me, dh, *blocks, *before, *[x for x, _ in terms])
    return result[-2:], (result[0] if terms else None)


def halves_kernel(me_ref, own_ref, came_ref, kept_ref, sent_ref):
    core = me_ref[0] % 2
    rows = kept_ref.shape[0]
    for ref, number in ((kept_ref, core), (sent_ref, 1 - core)):
        here = pl.ds(pl.multiple_of(number * rows, rows), rows)
        both = own_ref[here, :].astype(jnp.float32) + came_ref[here, :].astype(jnp.float32)
        ref[...] = both.astype(ref.dtype)


def halves(me, own, came):
    shape = (own.shape[0] // 2, own.shape[1])
    return pl.pallas_call(
        halves_kernel,
        out_shape=(
            jax.ShapeDtypeStruct(shape, jnp.float32),
            jax.ShapeDtypeStruct(shape, jnp.bfloat16),
        ),
        in_specs=[SCALAR, WHOLE, WHOLE],
        out_specs=(WHOLE, WHOLE),
        compiler_params=pltpu.CompilerParams(vmem_limit_bytes=VMEM_LIMIT),
        cost_estimate=cost(0.3),
        name="halves",
    )(me, own, came)


def last_kernel(me_ref, mine_ref, mine_came_ref, other_ref, other_came_ref, out_ref):
    core = me_ref[0] % 2
    half = mine_ref.shape[1]
    pairs = ((core, mine_ref, mine_came_ref), (1 - core, other_ref, other_came_ref))
    for number, kept, came in pairs:
        here = pl.ds(pl.multiple_of(number * half, half), half)
        out_ref[:, here] = (kept[...] + came[...].astype(jnp.float32)).astype(out_ref.dtype)


def last(me, mine, mine_came, other, other_came):
    shape = (mine.shape[0], 2 * mine.shape[1])
    return pl.pallas_call(
        last_kernel,
        out_shape=jax.ShapeDtypeStruct(shape, jnp.bfloat16),
        in_specs=[SCALAR] + [WHOLE] * 4,
        out_specs=WHOLE,
        compiler_params=pltpu.CompilerParams(vmem_limit_bytes=VMEM_LIMIT),
        cost_estimate=cost(0.3),
        name="last",
    )(me, mine, mine_came, other, other_came)


def total(*terms):
    result = terms[0].astype(jnp.float32)
    for term in terms[1:]:
        result = result + term.astype(jnp.float32)
    return result.astype(jnp.bfloat16)


def after(x, *others):
    return lax.optimization_barrier((x, *others))[0]


def on_device(out_grad, pre_act, layer_input, weight):
    n = lax.axis_size("gx")
    rows, width = layer_input.shape
    if n != 2 * RING or rows % 16 or width % (2 * PIECES * PIECE_STEPS * 128):
        return plain(out_grad, pre_act, layer_input, weight)

    pairs = ring_pairs()
    swaps = [(i, i ^ 1) for i in range(n)]

    def ring(x):
        return lax.ppermute(x, "gx", pairs)

    def swap(x):
        return lax.ppermute(x, "gx", swaps)

    out_grad, pre_act, own, weight = (
        pltpu.with_memory_space_constraint(x, pltpu.HBM)
        for x in (out_grad, pre_act, layer_input, weight)
    )
    me = lax.axis_index("gx").astype(jnp.int32).reshape(1)
    both = 2 * rows

    def block(x, k):
        return x[(k - 1) * both : k * both]

    def swap_blocks(x):
        return [swap(block(x, k)) for k in (1, 2, 3)]

    twin = swap(layer_input)
    m0, o0 = prepare(me, fetch(own), twin)

    def product(other, piece, w, before, *ties):
        return input_piece(me, after(dht, *ties), w, weight, before, other, piece)

    m1 = ring(m0)
    o1 = ring(o0)
    dh, dht, w = hidden(after(me, o0), out_grad, pre_act, weight)
    m1 = after(m1, dh)
    m2, sm1 = ring(m1), swap(m1)
    go, w = product(True, 0, w, (), m1)
    o1 = after(o1, go[0])
    o2, so1 = ring(o1), swap(o1)
    go, w = product(True, 1, w, go, o1)
    m2 = after(m2, go[0])
    m3, sm2 = ring(m2), swap(m2)
    go, w = product(True, 2, w, go, m2)
    o2 = after(o2, go[0])
    o3, so2 = ring(o2), swap(o2)
    go, w = product(True, 3, w, go, o2)
    m3 = after(m3, go[0])
    m4, sm3 = ring(m3), swap(m3)
    gm, w = product(False, 0, w, (), m3, so1)
    own_o, behind_o, opposite_o, ahead_o = go
    from_m, opposite_from = swap_blocks(behind_o), swap(opposite_o)
    gm, w = product(False, 1, w, gm, so2)
    o3 = after(o3, gm[0])
    so3 = swap(o3)
    gm, w = product(False, 2, w, gm, o3)
    m4 = after(m4, gm[0])
    sm4 = swap(m4)
    gm, _ = product(False, 3, w, gm, m4, *from_m, opposite_from)
    own_m, behind_m, opposite_m, ahead_m = gm
    r4m = ring(total(opposite_m, opposite_from))
    from_o = swap_blocks(behind_m)
    mine = (m0, m1, m2, m3, m4, so1, so2, so3)
    others = (o0, o1, o2, o3, sm4, sm1, sm2, sm3)

    def gradient(other, piece, before, *terms):
        blocks = others if other else mine
        before = before[::-1]
        return weight_piece(me, dh, blocks, before, other, piece, terms)

    gw, sent = gradient(False, 0, (), (ahead_o, 2), (from_o[2], 0))
    r3o = ring(sent)
    gw, sent = gradient(False, 1, gw, (ahead_m, 2), (from_m[2], 0), (r4m, 0))
    r3m = ring(sent)
    gw, sent = gradient(False, 2, gw, (ahead_o, 1), (from_o[1], 0), (r3o, 0))
    r2o = ring(sent)
    gw, sent = gradient(False, 3, gw, (ahead_m, 1), (from_m[1], 0), (r3m, 0))
    r2m = ring(sent)
    gw, sent = gradient(True, 0, gw, (ahead_o, 0), (from_o[0], 0), (r2o, 0))
    r1o = ring(sent)
    gw, sent = gradient(True, 1, gw, (ahead_m, 0), (from_m[0], 0), (r2m, 0))
    r1m = ring(sent)
    gw, _ = gradient(True, 2, gw)
    kept_o, sent_o = halves(me, own_o, after(r1o, gw[1]))
    came_m = swap(sent_o)
    gw, _ = gradient(True, 3, gw)
    kept_m, sent_m = halves(me, own_m, after(r1m, gw[1]))
    came_o = swap(sent_m)
    return (last(me, kept_m, came_m, kept_o, came_o), gw[0])


def solution(mesh):
    placed = (P("group", "gx"), P("group", "gx"), P(("group", "gx"), None), P(None, "gx"))
    return jax.shard_map(
        on_device,
        mesh=mesh,
        in_specs=placed,
        out_specs=(P(("group", "gx"), None), P(None, ("group", "gx"))),
        check_vma=False,
    )
```

```python
import math

import jax
import jax.numpy as jnp
from jax import lax
from jax.experimental import pallas as pl
from jax.experimental.pallas import tpu as pltpu
from jax.sharding import PartitionSpec as P

RING = 8
PIECE_STEPS = 2
PIECE_COST = 0.1
PIECES = 4
VMEM_LIMIT = 16 * 1024 * 1024
WHOLE = pl.BlockSpec(memory_space=pltpu.VMEM)
OUTSIDE = pl.BlockSpec(memory_space=pltpu.HBM)


def cost(microseconds):
    return pl.CostEstimate(
        flops=int(microseconds * 1.15e9), bytes_accessed=0, transcendentals=0
    )


ANYWHERE = pl.BlockSpec(memory_space=pl.ANY)
SCALAR = pl.BlockSpec(memory_space=pltpu.SMEM)


def gelu_slope(pre):
    coeff = math.sqrt(2.0 / math.pi)
    square = pre * pre
    tanh_value = jnp.tanh(pre * (coeff + coeff * 0.044715 * square))
    inner_slope = coeff + 3.0 * 0.044715 * coeff * square
    return (0.5 + 0.5 * tanh_value) * (1.0 + pre * (1.0 - tanh_value) * inner_slope)


def plain(out_grad, pre_act, layer_input, weight):
    slope = gelu_slope(pre_act.astype(jnp.float32))
    grad_hidden = (out_grad.astype(jnp.float32) * slope).astype(jnp.bfloat16)
    local_grad = lax.dot_general(
        lax.all_gather(layer_input, "gx", axis=0, tiled=True),
        grad_hidden,
        (((0,), (0,)), ((), ())),
        preferred_element_type=jnp.float32,
    )
    grad_input = lax.psum_scatter(
        lax.dot_general(
            grad_hidden, weight, (((1,), (1,)), ((), ())), preferred_element_type=jnp.float32
        ),
        "gx",
        scatter_dimension=0,
        tiled=True,
    ).astype(jnp.bfloat16)
    return (grad_input, local_grad.astype(jnp.bfloat16))


def chip_at(place):
    place = place & (RING - 1)
    return jnp.where(place < RING // 2, 2 * place, 2 * (RING - 1 - place) + 1)


def place_of(chip):
    return jnp.where(chip % 2 == 0, chip // 2, RING - 1 - chip // 2)


def ring_pairs():
    path = [2 * p if p < RING // 2 else 2 * (RING - 1 - p) + 1 for p in range(RING)]
    along, across = [], []
    for place, chip in enumerate(path):
        ahead, behind = path[(place + 1) % RING], path[(place - 1) % RING]
        along += [(2 * chip, 2 * ahead), (2 * chip + 1, 2 * behind + 1)]
        across += [(2 * chip, 2 * behind + 1), (2 * chip + 1, 2 * ahead)]
    return along, across


def chip_order(me):
    way = jnp.where(me % 2 == 0, 1, -1)
    place = place_of(me // 2)
    steps = [0, -1, -2, -3, 4, 1, 2, 3]
    return [chip_at(place + way * s + RING) for s in steps]


def hidden_kernel(me_ref, og_hbm, pre_hbm, w_hbm, dh_ref, dht_ref, w_ref, og_ref, pre_ref, sems):
    rows = dh_ref.shape[0] // (2 * RING)
    me = me_ref[0]
    copies = []
    for i, chip in enumerate(chip_order(me)):
        for j, core in enumerate((me % 2, 1 - me % 2)):
            source = pl.ds(pl.multiple_of((2 * chip + core) * rows, rows), rows)
            block = pl.ds((2 * i + j) * rows, rows)
            for k, (hbm, ref) in enumerate(((og_hbm, og_ref), (pre_hbm, pre_ref))):
                copy = pltpu.make_async_copy(
                    hbm.at[source, :], ref.at[block, :], sems.at[k, 2 * i + j]
                )
                copy.start()
                copies.append(copy)
    wide = w_ref.shape[0]
    first = first_row(me_ref, True, 0, w_hbm.shape[0] // 2, wide)
    fetch = pltpu.make_async_copy(w_hbm.at[pl.ds(first, wide), :], w_ref, sems.at[2, 0])
    fetch.start()
    for i in range(RING // 2):
        for copy in copies[8 * i : 8 * (i + 1)]:
            copy.wait()
        block = pl.ds(4 * i * rows, 4 * rows)
        pre = pre_ref[block, :].astype(jnp.float32)
        og = og_ref[block, :].astype(jnp.float32)
        dh = (og * gelu_slope(pre)).astype(jnp.bfloat16)
        dh_ref[block, :] = dh
        dht_ref[:, block] = dh.T
    fetch.wait()


def hidden(me, out_grad, pre_act, weight):
    shape, dtype = out_grad.shape, out_grad.dtype
    return pl.pallas_call(
        hidden_kernel,
        out_shape=(
            jax.ShapeDtypeStruct(shape, dtype),
            jax.ShapeDtypeStruct(shape[::-1], dtype),
            jax.ShapeDtypeStruct((weight.shape[0] // (2 * PIECES), shape[1]), dtype),
        ),
        in_specs=[SCALAR, OUTSIDE, OUTSIDE, OUTSIDE],
        out_specs=(WHOLE, WHOLE, WHOLE),
        scratch_shapes=[
            pltpu.VMEM(shape, dtype),
            pltpu.VMEM(shape, dtype),
            pltpu.SemaphoreType.DMA((3, 2 * RING)),
        ],
        compiler_params=pltpu.CompilerParams(vmem_limit_bytes=VMEM_LIMIT),
        cost_estimate=cost(1),
        name="hidden",
    )(me, out_grad, pre_act, weight)


def first_row(me_ref, other, piece, half, wide):
    core = me_ref[0] % 2
    number = 1 - core if other else core
    return pl.multiple_of(number * half + piece * wide, wide)


def input_kernel(me_ref, dht_ref, w_ref, w_hbm, *refs, other, piece, wide, more):
    outs, part_ref, sems = refs[-(RING + 2 + more) :][:RING], refs[-2], refs[-1]
    half = outs[0].shape[1]
    if more:
        following = (other, piece + 1) if piece + 1 < PIECES else (False, 0)
        fetch = pltpu.make_async_copy(
            w_hbm.at[pl.ds(first_row(me_ref, *following, half, wide), wide), :],
            refs[-3],
            sems.at[PIECE_STEPS, 0],
        )
        fetch.start()
    steps = PIECE_STEPS if other else 1
    step = wide // steps
    stores = []
    for i in range(steps):
        here = pl.ds(i * step, step)
        part = jnp.dot(w_ref[here, :], dht_ref[...], preferred_element_type=jnp.float32)
        part_ref[:, here] = part.astype(jnp.bfloat16).T
        for j, out in enumerate(outs):
            rows = out.shape[0]
            store = pltpu.make_async_copy(
                part_ref.at[pl.ds(j * rows, rows), here],
                out.at[:, pl.ds(piece * wide + i * step, step)],
                sems.at[i, j],
            )
            store.start()
            stores.append(store)
    for store in stores:
        store.wait()
    if more:
        fetch.wait()


def input_piece(me, dht, w, weight, before, other, piece):
    ff, tokens = dht.shape
    half = weight.shape[0] // 2
    wide = half // PIECES
    rows = tokens // RING
    more = other or piece + 1 < PIECES
    outs = (jax.ShapeDtypeStruct((rows, half), jnp.bfloat16),) * RING
    following = (jax.ShapeDtypeStruct((wide, ff), jnp.bfloat16),) if more else ()
    result = pl.pallas_call(
        lambda *refs: input_kernel(*refs, other=other, piece=piece, wide=wide, more=more),
        out_shape=outs + following,
        in_specs=[SCALAR, WHOLE, WHOLE, OUTSIDE] + [ANYWHERE] * len(before),
        out_specs=(ANYWHERE,) * RING + (WHOLE,) * len(following),
        input_output_aliases={4 + i: i for i in range(len(before))},
        scratch_shapes=[
            pltpu.VMEM((tokens, wide), jnp.bfloat16),
            pltpu.SemaphoreType.DMA((PIECE_STEPS + 1, RING)),
        ],
        compiler_params=pltpu.CompilerParams(vmem_limit_bytes=VMEM_LIMIT),
        cost_estimate=cost(PIECE_COST),
        name="input_piece",
    )(me, dht, w, weight, *before)
    return result[:RING], (result[RING] if more else None)


def weight_kernel(dh_ref, *refs, piece, wide, step):
    blocks, refs = refs[: 2 * RING], refs[2 * RING :]
    out_hbm, stage, sems = refs[-3:]
    width, columns = out_hbm.shape
    copies = []

    def store(source, number, i):
        here = pl.ds(i * step, step)
        rows = pl.ds(number * wide, wide)
        copy = pltpu.make_async_copy(
            source.at[:, here], out_hbm.at[rows, here], sems.at[piece - number, i]
        )
        copy.start()
        copies.append(copy)

    if piece:
        for i in range(columns // step):
            store(refs[0], piece - 1, i)
    x = jnp.concatenate([b[:, pl.ds(piece * wide, wide)] for b in blocks], axis=0).T
    for i in range(columns // step):
        here = pl.ds(i * step, step)
        stage[:, here] = jnp.dot(
            x, dh_ref[:, here], preferred_element_type=jnp.float32
        ).astype(jnp.bfloat16)
        if (piece + 1) * wide == width:
            store(stage, piece, i)
    for copy in copies:
        copy.wait()


def weight_piece(dh, blocks, before, piece):
    tokens, ff = dh.shape
    width = blocks[0].shape[1]
    wide = width // (2 * PIECES)
    step = 512 if ff % 512 == 0 else 128
    ends = piece == 2 * PIECES - 1
    stage = jax.ShapeDtypeStruct((wide, ff), jnp.bfloat16)
    return pl.pallas_call(
        lambda *refs: weight_kernel(*refs, piece=piece, wide=wide, step=step),
        out_shape=(jax.ShapeDtypeStruct((width, ff), jnp.bfloat16),) + (stage,) * (not ends),
        in_specs=[WHOLE] * (1 + 2 * RING) + ([WHOLE, OUTSIDE] if before else []),
        out_specs=(OUTSIDE,) + (WHOLE,) * (not ends),
        input_output_aliases={2 + 2 * RING: 0} if before else {},
        scratch_shapes=[pltpu.VMEM(stage.shape, stage.dtype)] * ends
        + [pltpu.SemaphoreType.DMA((2, ff // step))],
        compiler_params=pltpu.CompilerParams(vmem_limit_bytes=VMEM_LIMIT),
        cost_estimate=cost(PIECE_COST),
        name="weight_piece",
    )(dh, *blocks, *before)


def total_kernel(part_ref, twin_ref, *refs):
    rows = part_ref.shape[0] // 2
    for here, there in ((pl.ds(0, rows), pl.ds(rows, rows)), (pl.ds(rows, rows), pl.ds(0, rows))):
        total = part_ref[here, :].astype(jnp.float32) + twin_ref[there, :].astype(jnp.float32)
        for ref in refs[:-1]:
            total = total + ref[here, :].astype(jnp.float32)
        refs[-1][here, :] = total.astype(refs[-1].dtype)


def total(*terms):
    return pl.pallas_call(
        total_kernel,
        out_shape=jax.ShapeDtypeStruct(terms[0].shape, terms[0].dtype),
        in_specs=[WHOLE] * len(terms),
        out_specs=WHOLE,
        compiler_params=pltpu.CompilerParams(vmem_limit_bytes=VMEM_LIMIT),
        cost_estimate=cost(0.1),
        name="total",
    )(*terms)


def halves_kernel(own_ref, came_ref, kept_ref, sent_ref):
    rows = kept_ref.shape[0]
    for ref, here in ((kept_ref, pl.ds(0, rows)), (sent_ref, pl.ds(rows, rows))):
        both = own_ref[here, :].astype(jnp.float32) + came_ref[here, :].astype(jnp.float32)
        ref[...] = both.astype(ref.dtype)


def halves(own, came):
    shape = (own.shape[0] // 2, own.shape[1])
    return pl.pallas_call(
        halves_kernel,
        out_shape=(
            jax.ShapeDtypeStruct(shape, jnp.float32),
            jax.ShapeDtypeStruct(shape, jnp.bfloat16),
        ),
        in_specs=[WHOLE, WHOLE],
        out_specs=(WHOLE, WHOLE),
        compiler_params=pltpu.CompilerParams(vmem_limit_bytes=VMEM_LIMIT),
        cost_estimate=cost(0.1),
        name="halves",
    )(own, came)


def last_kernel(me_ref, mine_ref, mine_came_ref, other_ref, other_came_ref, out_ref):
    core = me_ref[0] % 2
    half = mine_ref.shape[1]
    pairs = ((core, mine_ref, mine_came_ref), (1 - core, other_ref, other_came_ref))
    for number, kept, came in pairs:
        here = pl.ds(pl.multiple_of(number * half, half), half)
        out_ref[:, here] = (kept[...] + came[...].astype(jnp.float32)).astype(out_ref.dtype)


def last(me, mine, mine_came, other, other_came):
    shape = (mine.shape[0], 2 * mine.shape[1])
    return pl.pallas_call(
        last_kernel,
        out_shape=jax.ShapeDtypeStruct(shape, jnp.bfloat16),
        in_specs=[SCALAR] + [WHOLE] * 4,
        out_specs=WHOLE,
        compiler_params=pltpu.CompilerParams(vmem_limit_bytes=VMEM_LIMIT),
        cost_estimate=cost(0.3),
        name="last",
    )(me, mine, mine_came, other, other_came)


def after(x, *others):
    return lax.optimization_barrier((x, *others))[0]


def on_device(out_grad, pre_act, layer_input, weight):
    n = lax.axis_size("gx")
    rows, width = layer_input.shape
    if n != 2 * RING or rows % 16 or width % (2 * PIECES * PIECE_STEPS * 128):
        return plain(out_grad, pre_act, layer_input, weight)

    along, across = ring_pairs()
    twins = [(i, i ^ 1) for i in range(n)]

    def ring(x):
        return lax.ppermute(x, "gx", along)

    def swap(x):
        return lax.ppermute(x, "gx", twins)

    out_grad, pre_act, weight = (
        pltpu.with_memory_space_constraint(x, pltpu.HBM) for x in (out_grad, pre_act, weight)
    )
    me = lax.axis_index("gx").astype(jnp.int32).reshape(1)

    a1, b1 = ring(layer_input), lax.ppermute(layer_input, "gx", across)
    twin = swap(layer_input)
    dh, dht, w = hidden(me, out_grad, pre_act, weight)

    def product(other, piece, w, before, *ties):
        return input_piece(me, after(dht, *ties), w, weight, before, other, piece)

    a1 = after(a1, dh)
    a2, sa1 = ring(a1), swap(a1)
    go, w = product(True, 0, w, (), a1, twin)
    b1 = after(b1, go[0])
    b2, sb1 = ring(b1), swap(b1)
    go, w = product(True, 1, w, go, b1, sa1)
    a2 = after(a2, go[0])
    a3, sa2 = ring(a2), swap(a2)
    go, w = product(True, 2, w, go, a2, sb1)
    b2 = after(b2, go[0])
    b3, sb2 = ring(b2), swap(b2)
    go, w = product(True, 3, w, go, b2, sa2)
    a3 = after(a3, go[0])
    a4, sa3 = ring(a3), swap(a3)
    gm, w = product(False, 0, w, (), a3, sb2)
    own_o, behind_o, opposite_o, ahead_o = go[0], go[1:4], go[4], go[5:]
    from_m, opposite_from = [swap(x) for x in behind_o], swap(opposite_o)
    gm, w = product(False, 1, w, gm, sa3)
    b3 = after(b3, gm[0])
    sb3 = swap(b3)
    gm, w = product(False, 2, w, gm, b3, *from_m)
    a4 = after(a4, gm[0])
    sa4 = swap(a4)
    gm, _ = product(False, 3, w, gm, a4, sb3, opposite_from)
    own_m, behind_m, opposite_m, ahead_m = gm[0], gm[1:4], gm[4], gm[5:]
    sent = total(opposite_m, opposite_from)
    r4m = ring(sent)
    from_o = [swap(after(x, sent)) for x in behind_m[::-1]][::-1]
    blocks = (layer_input, twin, a1, b1, a2, b2, a3, b3, a4, sa4, sb1, sa1, sb2, sa2, sb3, sa3)

    def gradient(piece, before, *ties):
        before = before[::-1]
        return weight_piece(after(dh, *ties), blocks, before, piece)

    def send(k, ahead, came, *ring_terms):
        return total(ahead[k - 1], came[k - 1], *ring_terms)

    gw = gradient(0, (), sent, from_o[2])
    sent = send(3, ahead_o, from_o[:2] + [after(from_o[2], gw[1])])
    r3o = ring(sent)
    gw = gradient(1, gw, sent, from_o[1])
    sent = send(3, ahead_m, from_m, after(r4m, gw[1]))
    r3m = ring(sent)
    gw = gradient(2, gw, sent, from_o[0])
    sent = send(2, ahead_o, from_o, after(r3o, gw[1]))
    r2o = ring(sent)
    gw = gradient(3, gw, sent)
    sent = send(2, ahead_m, from_m, after(r3m, gw[1]))
    r2m = ring(sent)
    gw = gradient(4, gw, sent)
    sent = send(1, ahead_o, from_o, after(r2o, gw[1]))
    r1o = ring(sent)
    gw = gradient(5, gw, sent)
    sent = send(1, ahead_m, from_m, after(r2m, gw[1]))
    r1m = ring(sent)
    gw = gradient(6, gw, sent)
    kept_o, sent_o = halves(own_o, after(r1o, gw[1]))
    came_m = swap(sent_o)
    gw = gradient(7, gw, sent_o)
    kept_m, sent_m = halves(own_m, after(r1m, gw[0]))
    came_o = swap(sent_m)
    return (last(me, kept_m, came_m, kept_o, came_o), gw[0])


def solution(mesh):
    placed = (P("group", "gx"), P("group", "gx"), P(("group", "gx"), None), P(None, "gx"))
    return jax.shard_map(
        on_device,
        mesh=mesh,
        in_specs=placed,
        out_specs=(P(("group", "gx"), None), P(None, ("group", "gx"))),
        check_vma=False,
    )
```

```python
import math

import jax
import jax.numpy as jnp
from jax import lax
from jax.experimental import pallas as pl
from jax.experimental.pallas import tpu as pltpu
from jax.sharding import PartitionSpec as P

RING = 8
PIECE_STEPS = 1
PIECE_COST = 0.1
PIECES = 4
VMEM_LIMIT = 16 * 1024 * 1024
WHOLE = pl.BlockSpec(memory_space=pltpu.VMEM)
OUTSIDE = pl.BlockSpec(memory_space=pltpu.HBM)


def cost(microseconds):
    return pl.CostEstimate(
        flops=int(microseconds * 1.15e9), bytes_accessed=0, transcendentals=0
    )


ANYWHERE = pl.BlockSpec(memory_space=pl.ANY)
SCALAR = pl.BlockSpec(memory_space=pltpu.SMEM)


def gelu_slope(pre):
    coeff = math.sqrt(2.0 / math.pi)
    square = pre * pre
    tanh_value = jnp.tanh(pre * (coeff + coeff * 0.044715 * square))
    inner_slope = coeff + 3.0 * 0.044715 * coeff * square
    return (0.5 + 0.5 * tanh_value) * (1.0 + pre * (1.0 - tanh_value) * inner_slope)


def plain(out_grad, pre_act, layer_input, weight):
    slope = gelu_slope(pre_act.astype(jnp.float32))
    grad_hidden = (out_grad.astype(jnp.float32) * slope).astype(jnp.bfloat16)
    local_grad = lax.dot_general(
        lax.all_gather(layer_input, "gx", axis=0, tiled=True),
        grad_hidden,
        (((0,), (0,)), ((), ())),
        preferred_element_type=jnp.float32,
    )
    grad_input = lax.psum_scatter(
        lax.dot_general(
            grad_hidden, weight, (((1,), (1,)), ((), ())), preferred_element_type=jnp.float32
        ),
        "gx",
        scatter_dimension=0,
        tiled=True,
    ).astype(jnp.bfloat16)
    return (grad_input, local_grad.astype(jnp.bfloat16))


def chip_at(place):
    place = place & (RING - 1)
    return jnp.where(place < RING // 2, 2 * place, 2 * (RING - 1 - place) + 1)


def place_of(chip):
    return jnp.where(chip % 2 == 0, chip // 2, RING - 1 - chip // 2)


def ring_pairs():
    path = [2 * p if p < RING // 2 else 2 * (RING - 1 - p) + 1 for p in range(RING)]
    along, across = [], []
    for place, chip in enumerate(path):
        ahead, behind = path[(place + 1) % RING], path[(place - 1) % RING]
        along += [(2 * chip, 2 * ahead), (2 * chip + 1, 2 * behind + 1)]
        across += [(2 * chip, 2 * behind + 1), (2 * chip + 1, 2 * ahead)]
    return along, across


def chip_order(me):
    way = jnp.where(me % 2 == 0, 1, -1)
    place = place_of(me // 2)
    steps = [0, -1, -2, -3, 4, 1, 2, 3]
    return [chip_at(place + way * s + RING) for s in steps]


def hidden_kernel(me_ref, og_hbm, pre_hbm, w_hbm, dh_ref, dht_ref, w_ref, og_ref, pre_ref, sems):
    rows = dh_ref.shape[0] // (2 * RING)
    me = me_ref[0]
    copies = []
    for i, chip in enumerate(chip_order(me)):
        for j, core in enumerate((me % 2, 1 - me % 2)):
            source = pl.ds(pl.multiple_of((2 * chip + core) * rows, rows), rows)
            block = pl.ds((2 * i + j) * rows, rows)
            for k, (hbm, ref) in enumerate(((og_hbm, og_ref), (pre_hbm, pre_ref))):
                copy = pltpu.make_async_copy(
                    hbm.at[source, :], ref.at[block, :], sems.at[k, 2 * i + j]
                )
                copy.start()
                copies.append(copy)
    wide = w_ref.shape[0]
    first = first_row(me_ref, True, 0, w_hbm.shape[0] // 2, wide)
    fetch = pltpu.make_async_copy(w_hbm.at[pl.ds(first, wide), :], w_ref, sems.at[2, 0])
    fetch.start()
    for i in range(RING // 2):
        for copy in copies[8 * i : 8 * (i + 1)]:
            copy.wait()
        block = pl.ds(4 * i * rows, 4 * rows)
        pre = pre_ref[block, :].astype(jnp.float32)
        og = og_ref[block, :].astype(jnp.float32)
        dh = (og * gelu_slope(pre)).astype(jnp.bfloat16)
        dh_ref[block, :] = dh
        dht_ref[:, block] = dh.T
    fetch.wait()


def hidden(me, out_grad, pre_act, weight):
    shape, dtype = out_grad.shape, out_grad.dtype
    return pl.pallas_call(
        hidden_kernel,
        out_shape=(
            jax.ShapeDtypeStruct(shape, dtype),
            jax.ShapeDtypeStruct(shape[::-1], dtype),
            jax.ShapeDtypeStruct((weight.shape[0] // (2 * PIECES), shape[1]), dtype),
        ),
        in_specs=[SCALAR, OUTSIDE, OUTSIDE, OUTSIDE],
        out_specs=(WHOLE, WHOLE, WHOLE),
        scratch_shapes=[
            pltpu.VMEM(shape, dtype),
            pltpu.VMEM(shape, dtype),
            pltpu.SemaphoreType.DMA((3, 2 * RING)),
        ],
        compiler_params=pltpu.CompilerParams(vmem_limit_bytes=VMEM_LIMIT),
        cost_estimate=cost(1),
        name="hidden",
    )(me, out_grad, pre_act, weight)


def first_row(me_ref, other, piece, half, wide):
    core = me_ref[0] % 2
    number = 1 - core if other else core
    return pl.multiple_of(number * half + piece * wide, wide)


def input_kernel(me_ref, dht_ref, w_ref, w_hbm, *refs, other, piece, wide, more):
    outs, part_ref, sems = refs[-(RING + 2 + more) :][:RING], refs[-2], refs[-1]
    half = outs[0].shape[1]
    if more:
        following = (other, piece + 1) if piece + 1 < PIECES else (False, 0)
        fetch = pltpu.make_async_copy(
            w_hbm.at[pl.ds(first_row(me_ref, *following, half, wide), wide), :],
            refs[-3],
            sems.at[PIECE_STEPS, 0],
        )
        fetch.start()
    step = wide // PIECE_STEPS
    stores = []
    for i in range(PIECE_STEPS):
        here = pl.ds(i * step, step)
        part = jnp.dot(w_ref[here, :], dht_ref[...], preferred_element_type=jnp.float32)
        part_ref[:, here] = part.astype(jnp.bfloat16).T
        for j, out in enumerate(outs):
            rows = out.shape[0]
            store = pltpu.make_async_copy(
                part_ref.at[pl.ds(j * rows, rows), here],
                out.at[:, pl.ds(piece * wide + i * step, step)],
                sems.at[i, j],
            )
            store.start()
            stores.append(store)
    for store in stores:
        store.wait()
    if more:
        fetch.wait()


def input_piece(me, dht, w, weight, before, other, piece):
    ff, tokens = dht.shape
    half = weight.shape[0] // 2
    wide = half // PIECES
    rows = tokens // RING
    more = other or piece + 1 < PIECES
    outs = (jax.ShapeDtypeStruct((rows, half), jnp.bfloat16),) * RING
    following = (jax.ShapeDtypeStruct((wide, ff), jnp.bfloat16),) if more else ()
    result = pl.pallas_call(
        lambda *refs: input_kernel(*refs, other=other, piece=piece, wide=wide, more=more),
        out_shape=outs + following,
        in_specs=[SCALAR, WHOLE, WHOLE, OUTSIDE] + [ANYWHERE] * len(before),
        out_specs=(ANYWHERE,) * RING + (WHOLE,) * len(following),
        input_output_aliases={4 + i: i for i in range(len(before))},
        scratch_shapes=[
            pltpu.VMEM((tokens, wide), jnp.bfloat16),
            pltpu.SemaphoreType.DMA((PIECE_STEPS + 1, RING)),
        ],
        compiler_params=pltpu.CompilerParams(vmem_limit_bytes=VMEM_LIMIT),
        cost_estimate=cost(PIECE_COST),
        name="input_piece",
    )(me, dht, w, weight, *before)
    return result[:RING], (result[RING] if more else None)


def weight_kernel(dh_ref, *refs, piece, wide, step):
    blocks, refs = refs[: 2 * RING], refs[2 * RING :]
    out_hbm, stage, sems = refs[-3:]
    width, columns = out_hbm.shape
    copies = []

    def store(source, number, i):
        here = pl.ds(i * step, step)
        rows = pl.ds(number * wide, wide)
        copy = pltpu.make_async_copy(
            source.at[:, here], out_hbm.at[rows, here], sems.at[piece - number, i]
        )
        copy.start()
        copies.append(copy)

    if piece:
        for i in range(columns // step):
            store(refs[0], piece - 1, i)
    x = jnp.concatenate([b[:, pl.ds(piece * wide, wide)] for b in blocks], axis=0).T
    for i in range(columns // step):
        here = pl.ds(i * step, step)
        stage[:, here] = jnp.dot(
            x, dh_ref[:, here], preferred_element_type=jnp.float32
        ).astype(jnp.bfloat16)
        if (piece + 1) * wide == width:
            store(stage, piece, i)
    for copy in copies:
        copy.wait()


def weight_piece(dh, blocks, before, piece):
    tokens, ff = dh.shape
    width = blocks[0].shape[1]
    wide = width // (2 * PIECES)
    step = 512 if ff % 512 == 0 else 128
    ends = piece == 2 * PIECES - 1
    stage = jax.ShapeDtypeStruct((wide, ff), jnp.bfloat16)
    return pl.pallas_call(
        lambda *refs: weight_kernel(*refs, piece=piece, wide=wide, step=step),
        out_shape=(jax.ShapeDtypeStruct((width, ff), jnp.bfloat16),) + (stage,) * (not ends),
        in_specs=[WHOLE] * (1 + 2 * RING) + ([WHOLE, OUTSIDE] if before else []),
        out_specs=(OUTSIDE,) + (WHOLE,) * (not ends),
        input_output_aliases={2 + 2 * RING: 0} if before else {},
        scratch_shapes=[pltpu.VMEM(stage.shape, stage.dtype)] * ends
        + [pltpu.SemaphoreType.DMA((2, ff // step))],
        compiler_params=pltpu.CompilerParams(vmem_limit_bytes=VMEM_LIMIT),
        cost_estimate=cost(PIECE_COST),
        name="weight_piece",
    )(dh, *blocks, *before)


def total_kernel(part_ref, twin_ref, *refs):
    rows = part_ref.shape[0] // 2
    for here, there in ((pl.ds(0, rows), pl.ds(rows, rows)), (pl.ds(rows, rows), pl.ds(0, rows))):
        total = part_ref[here, :].astype(jnp.float32) + twin_ref[there, :].astype(jnp.float32)
        for ref in refs[:-1]:
            total = total + ref[here, :].astype(jnp.float32)
        refs[-1][here, :] = total.astype(refs[-1].dtype)


def total(*terms):
    return pl.pallas_call(
        total_kernel,
        out_shape=jax.ShapeDtypeStruct(terms[0].shape, terms[0].dtype),
        in_specs=[WHOLE] * len(terms),
        out_specs=WHOLE,
        compiler_params=pltpu.CompilerParams(vmem_limit_bytes=VMEM_LIMIT),
        cost_estimate=cost(0.1),
        name="total",
    )(*terms)


def halves_kernel(own_ref, came_ref, kept_ref, sent_ref):
    rows = kept_ref.shape[0]
    for ref, here in ((kept_ref, pl.ds(0, rows)), (sent_ref, pl.ds(rows, rows))):
        both = own_ref[here, :].astype(jnp.float32) + came_ref[here, :].astype(jnp.float32)
        ref[...] = both.astype(ref.dtype)


def halves(own, came):
    shape = (own.shape[0] // 2, own.shape[1])
    return pl.pallas_call(
        halves_kernel,
        out_shape=(
            jax.ShapeDtypeStruct(shape, jnp.float32),
            jax.ShapeDtypeStruct(shape, jnp.bfloat16),
        ),
        in_specs=[WHOLE, WHOLE],
        out_specs=(WHOLE, WHOLE),
        compiler_params=pltpu.CompilerParams(vmem_limit_bytes=VMEM_LIMIT),
        cost_estimate=cost(0.1),
        name="halves",
    )(own, came)


def last_kernel(me_ref, mine_ref, mine_came_ref, other_ref, other_came_ref, out_ref):
    core = me_ref[0] % 2
    half = mine_ref.shape[1]
    pairs = ((core, mine_ref, mine_came_ref), (1 - core, other_ref, other_came_ref))
    for number, kept, came in pairs:
        here = pl.ds(pl.multiple_of(number * half, half), half)
        out_ref[:, here] = (kept[...] + came[...].astype(jnp.float32)).astype(out_ref.dtype)


def last(me, mine, mine_came, other, other_came):
    shape = (mine.shape[0], 2 * mine.shape[1])
    return pl.pallas_call(
        last_kernel,
        out_shape=jax.ShapeDtypeStruct(shape, jnp.bfloat16),
        in_specs=[SCALAR] + [WHOLE] * 4,
        out_specs=WHOLE,
        compiler_params=pltpu.CompilerParams(vmem_limit_bytes=VMEM_LIMIT),
        cost_estimate=cost(0.3),
        name="last",
    )(me, mine, mine_came, other, other_came)


def after(x, *others):
    return lax.optimization_barrier((x, *others))[0]


def on_device(out_grad, pre_act, layer_input, weight):
    n = lax.axis_size("gx")
    rows, width = layer_input.shape
    if n != 2 * RING or rows % 16 or width % (2 * PIECES * PIECE_STEPS * 128):
        return plain(out_grad, pre_act, layer_input, weight)

    along, across = ring_pairs()
    twins = [(i, i ^ 1) for i in range(n)]

    def ring(x):
        return lax.ppermute(x, "gx", along)

    def swap(x):
        return lax.ppermute(x, "gx", twins)

    out_grad, pre_act, weight = (
        pltpu.with_memory_space_constraint(x, pltpu.HBM) for x in (out_grad, pre_act, weight)
    )
    me = lax.axis_index("gx").astype(jnp.int32).reshape(1)

    a1, twin = ring(layer_input), swap(layer_input)
    dh, dht, w = hidden(me, out_grad, pre_act, weight)
    b1 = lax.ppermute(after(layer_input, dh), "gx", across)

    def product(other, piece, w, before, *ties):
        return input_piece(me, after(dht, *ties), w, weight, before, other, piece)

    go, w = product(True, 0, w, ())
    a1 = after(a1, go[0])
    a2, sa1 = ring(a1), swap(a1)
    go, w = product(True, 1, w, go, a1, twin)
    b1 = after(b1, go[0])
    b2, sb1 = ring(b1), swap(b1)
    go, w = product(True, 2, w, go, b1, sa1)
    a2 = after(a2, go[0])
    a3, sa2 = ring(a2), swap(a2)
    go, w = product(True, 3, w, go, a2, sb1)
    b2 = after(b2, go[0])
    b3, sb2 = ring(b2), swap(b2)
    gm, w = product(False, 0, w, (), b2, sa2)
    a3 = after(a3, gm[0])
    a4, sa3 = ring(a3), swap(a3)
    own_o, behind_o, opposite_o, ahead_o = go[0], go[1:4], go[4], go[5:]
    opposite_from = swap(opposite_o)
    gm, w = product(False, 1, w, gm, a3, sb2)
    gm, w = product(False, 2, w, gm, sa3, opposite_from)
    gm, _ = product(False, 3, w, gm, b3)
    own_m, behind_m, opposite_m, ahead_m = gm[0], gm[1:4], gm[4], gm[5:]
    sent = total(opposite_m, opposite_from)
    r4m = ring(sent)
    a4 = after(a4, sent)
    sa4 = swap(a4)
    from_o, from_m = [None] * 3, [None] * 3
    from_o[2], from_m[2] = swap(after(behind_m[2], sent)), swap(after(behind_o[2], sent))

    def gradient(piece, before, *ties):
        before = before[::-1]
        return weight_piece(after(dh, *ties), blocks, before, piece)

    def send(k, ahead, came, *ring_terms):
        return total(ahead[k - 1], came[k - 1], *ring_terms)

    sent = send(3, ahead_o, from_o)
    r3o = ring(sent)
    sb3 = swap(after(b3, sent))
    blocks = (layer_input, twin, a1, b1, a2, b2, a3, b3, a4, sa4, sb1, sa1, sb2, sa2, sb3, sa3)
    from_o[1], from_m[1] = swap(after(behind_m[1], sent)), swap(after(behind_o[1], sent))
    gw = gradient(0, (), sent)
    sent = send(3, ahead_m, from_m, after(r4m, gw[1]))
    r3m = ring(sent)
    from_o[0], from_m[0] = swap(after(behind_m[0], sent)), swap(after(behind_o[0], sent))
    gw = gradient(1, gw, sent, from_o[1], from_m[1])
    sent = send(2, ahead_o, from_o, after(r3o, gw[1]))
    r2o = ring(sent)
    gw = gradient(2, gw, sent, from_o[0], from_m[0])
    sent = send(2, ahead_m, from_m, after(r3m, gw[1]))
    r2m = ring(sent)
    gw = gradient(3, gw, sent)
    sent = send(1, ahead_o, from_o, after(r2o, gw[1]))
    r1o = ring(sent)
    gw = gradient(4, gw, sent)
    sent = send(1, ahead_m, from_m, after(r2m, gw[1]))
    r1m = ring(sent)
    gw = gradient(5, gw, sent)
    kept_o, sent_o = halves(own_o, after(r1o, gw[1]))
    came_m = swap(sent_o)
    gw = gradient(6, gw, sent_o)
    gw = gradient(7, gw, came_m)
    kept_m, sent_m = halves(own_m, after(r1m, gw[0]))
    came_o = swap(sent_m)
    return (last(me, kept_m, came_m, kept_o, came_o), gw[0])


def solution(mesh):
    placed = (P("group", "gx"), P("group", "gx"), P(("group", "gx"), None), P(None, "gx"))
    return jax.shard_map(
        on_device,
        mesh=mesh,
        in_specs=placed,
        out_specs=(P(("group", "gx"), None), P(None, ("group", "gx"))),
        check_vma=False,
    )
```

```python
import math

import jax
import jax.numpy as jnp
from jax import lax
from jax.experimental import pallas as pl
from jax.experimental.pallas import tpu as pltpu
from jax.sharding import PartitionSpec as P

RING = 8
PIECE_STEPS = 2
PIECE_COST = 0.1
PIECES = 4
VMEM_LIMIT = 16 * 1024 * 1024
WHOLE = pl.BlockSpec(memory_space=pltpu.VMEM)
OUTSIDE = pl.BlockSpec(memory_space=pltpu.HBM)


def cost(microseconds):
    return pl.CostEstimate(
        flops=int(microseconds * 1.15e9), bytes_accessed=0, transcendentals=0
    )


ANYWHERE = pl.BlockSpec(memory_space=pl.ANY)
SCALAR = pl.BlockSpec(memory_space=pltpu.SMEM)


def gelu_slope(pre):
    coeff = math.sqrt(2.0 / math.pi)
    square = pre * pre
    tanh_value = jnp.tanh(pre * (coeff + coeff * 0.044715 * square))
    inner_slope = coeff + 3.0 * 0.044715 * coeff * square
    return (0.5 + 0.5 * tanh_value) * (1.0 + pre * (1.0 - tanh_value) * inner_slope)


def plain(out_grad, pre_act, layer_input, weight):
    slope = gelu_slope(pre_act.astype(jnp.float32))
    grad_hidden = (out_grad.astype(jnp.float32) * slope).astype(jnp.bfloat16)
    local_grad = lax.dot_general(
        lax.all_gather(layer_input, "gx", axis=0, tiled=True),
        grad_hidden,
        (((0,), (0,)), ((), ())),
        preferred_element_type=jnp.float32,
    )
    grad_input = lax.psum_scatter(
        lax.dot_general(
            grad_hidden, weight, (((1,), (1,)), ((), ())), preferred_element_type=jnp.float32
        ),
        "gx",
        scatter_dimension=0,
        tiled=True,
    ).astype(jnp.bfloat16)
    return (grad_input, local_grad.astype(jnp.bfloat16))


def chip_at(place):
    place = place & (RING - 1)
    return jnp.where(place < RING // 2, 2 * place, 2 * (RING - 1 - place) + 1)


def place_of(chip):
    return jnp.where(chip % 2 == 0, chip // 2, RING - 1 - chip // 2)


def ring_pairs():
    path = [2 * p if p < RING // 2 else 2 * (RING - 1 - p) + 1 for p in range(RING)]
    along, across = [], []
    for place, chip in enumerate(path):
        ahead, behind = path[(place + 1) % RING], path[(place - 1) % RING]
        along += [(2 * chip, 2 * ahead), (2 * chip + 1, 2 * behind + 1)]
        across += [(2 * chip, 2 * behind + 1), (2 * chip + 1, 2 * ahead)]
    return along, across


def chip_order(me):
    way = jnp.where(me % 2 == 0, 1, -1)
    place = place_of(me // 2)
    steps = [0, -1, -2, -3, 4, 1, 2, 3]
    return [chip_at(place + way * s + RING) for s in steps]


def hidden_kernel(me_ref, og_hbm, pre_hbm, w_hbm, dh_ref, dht_ref, w_ref, og_ref, pre_ref, sems):
    rows = dh_ref.shape[0] // (2 * RING)
    me = me_ref[0]
    copies = []
    for i, chip in enumerate(chip_order(me)):
        for j, core in enumerate((me % 2, 1 - me % 2)):
            source = pl.ds(pl.multiple_of((2 * chip + core) * rows, rows), rows)
            block = pl.ds((2 * i + j) * rows, rows)
            for k, (hbm, ref) in enumerate(((og_hbm, og_ref), (pre_hbm, pre_ref))):
                copy = pltpu.make_async_copy(
                    hbm.at[source, :], ref.at[block, :], sems.at[k, 2 * i + j]
                )
                copy.start()
                copies.append(copy)
    wide = w_ref.shape[0]
    first = first_row(me_ref, True, 0, w_hbm.shape[0] // 2, wide)
    fetch = pltpu.make_async_copy(w_hbm.at[pl.ds(first, wide), :], w_ref, sems.at[2, 0])
    fetch.start()
    for i in range(RING // 2):
        for copy in copies[8 * i : 8 * (i + 1)]:
            copy.wait()
        block = pl.ds(4 * i * rows, 4 * rows)
        pre = pre_ref[block, :].astype(jnp.float32)
        og = og_ref[block, :].astype(jnp.float32)
        dh = (og * gelu_slope(pre)).astype(jnp.bfloat16)
        dh_ref[block, :] = dh
        dht_ref[:, block] = dh.T
    fetch.wait()


def hidden(me, out_grad, pre_act, weight):
    shape, dtype = out_grad.shape, out_grad.dtype
    return pl.pallas_call(
        hidden_kernel,
        out_shape=(
            jax.ShapeDtypeStruct(shape, dtype),
            jax.ShapeDtypeStruct(shape[::-1], dtype),
            jax.ShapeDtypeStruct((weight.shape[0] // (2 * PIECES), shape[1]), dtype),
        ),
        in_specs=[SCALAR, OUTSIDE, OUTSIDE, OUTSIDE],
        out_specs=(WHOLE, WHOLE, WHOLE),
        scratch_shapes=[
            pltpu.VMEM(shape, dtype),
            pltpu.VMEM(shape, dtype),
            pltpu.SemaphoreType.DMA((3, 2 * RING)),
        ],
        compiler_params=pltpu.CompilerParams(vmem_limit_bytes=VMEM_LIMIT),
        cost_estimate=cost(1),
        name="hidden",
    )(me, out_grad, pre_act, weight)


def first_row(me_ref, other, piece, half, wide):
    core = me_ref[0] % 2
    number = 1 - core if other else core
    return pl.multiple_of(number * half + piece * wide, wide)


def input_kernel(me_ref, dht_ref, w_ref, w_hbm, *refs, other, piece, wide, more):
    outs, part_ref, sems = refs[-(RING + 2 + more) :][:RING], refs[-2], refs[-1]
    half = outs[0].shape[1]
    if more:
        following = (other, piece + 1) if piece + 1 < PIECES else (False, 0)
        fetch = pltpu.make_async_copy(
            w_hbm.at[pl.ds(first_row(me_ref, *following, half, wide), wide), :],
            refs[-3],
            sems.at[PIECE_STEPS, 0],
        )
        fetch.start()
    steps = PIECE_STEPS if other else 1
    step = wide // steps
    stores = []
    for i in range(steps):
        here = pl.ds(i * step, step)
        part = jnp.dot(w_ref[here, :], dht_ref[...], preferred_element_type=jnp.float32)
        part_ref[:, here] = part.astype(jnp.bfloat16).T
        for j, out in enumerate(outs):
            rows = out.shape[0]
            store = pltpu.make_async_copy(
                part_ref.at[pl.ds(j * rows, rows), here],
                out.at[:, pl.ds(piece * wide + i * step, step)],
                sems.at[i, j],
            )
            store.start()
            stores.append(store)
    for store in stores:
        store.wait()
    if more:
        fetch.wait()


def input_piece(me, dht, w, weight, before, other, piece):
    ff, tokens = dht.shape
    half = weight.shape[0] // 2
    wide = half // PIECES
    rows = tokens // RING
    more = other or piece + 1 < PIECES
    outs = (jax.ShapeDtypeStruct((rows, half), jnp.bfloat16),) * RING
    following = (jax.ShapeDtypeStruct((wide, ff), jnp.bfloat16),) if more else ()
    result = pl.pallas_call(
        lambda *refs: input_kernel(*refs, other=other, piece=piece, wide=wide, more=more),
        out_shape=outs + following,
        in_specs=[SCALAR, WHOLE, WHOLE, OUTSIDE] + [ANYWHERE] * len(before),
        out_specs=(ANYWHERE,) * RING + (WHOLE,) * len(following),
        input_output_aliases={4 + i: i for i in range(len(before))},
        scratch_shapes=[
            pltpu.VMEM((tokens, wide), jnp.bfloat16),
            pltpu.SemaphoreType.DMA((PIECE_STEPS + 1, RING)),
        ],
        compiler_params=pltpu.CompilerParams(vmem_limit_bytes=VMEM_LIMIT),
        cost_estimate=cost(PIECE_COST),
        name="input_piece",
    )(me, dht, w, weight, *before)
    return result[:RING], (result[RING] if more else None)


def weight_kernel(dh_ref, *refs, piece, wide, step):
    blocks, refs = refs[: 2 * RING], refs[2 * RING :]
    out_hbm, stage, sems = refs[-3:]
    width, columns = out_hbm.shape
    copies = []

    def store(source, number, i):
        here = pl.ds(i * step, step)
        rows = pl.ds(number * wide, wide)
        copy = pltpu.make_async_copy(
            source.at[:, here], out_hbm.at[rows, here], sems.at[piece - number, i]
        )
        copy.start()
        copies.append(copy)

    if piece:
        for i in range(columns // step):
            store(refs[0], piece - 1, i)
    x = jnp.concatenate([b[:, pl.ds(piece * wide, wide)] for b in blocks], axis=0).T
    for i in range(columns // step):
        here = pl.ds(i * step, step)
        stage[:, here] = jnp.dot(
            x, dh_ref[:, here], preferred_element_type=jnp.float32
        ).astype(jnp.bfloat16)
        if (piece + 1) * wide == width:
            store(stage, piece, i)
    for copy in copies:
        copy.wait()


def weight_piece(dh, blocks, before, piece):
    tokens, ff = dh.shape
    width = blocks[0].shape[1]
    wide = width // (2 * PIECES)
    step = 512 if ff % 512 == 0 else 128
    ends = piece == 2 * PIECES - 1
    stage = jax.ShapeDtypeStruct((wide, ff), jnp.bfloat16)
    return pl.pallas_call(
        lambda *refs: weight_kernel(*refs, piece=piece, wide=wide, step=step),
        out_shape=(jax.ShapeDtypeStruct((width, ff), jnp.bfloat16),) + (stage,) * (not ends),
        in_specs=[WHOLE] * (1 + 2 * RING) + ([WHOLE, OUTSIDE] if before else []),
        out_specs=(OUTSIDE,) + (WHOLE,) * (not ends),
        input_output_aliases={2 + 2 * RING: 0} if before else {},
        scratch_shapes=[pltpu.VMEM(stage.shape, stage.dtype)] * ends
        + [pltpu.SemaphoreType.DMA((2, ff // step))],
        compiler_params=pltpu.CompilerParams(vmem_limit_bytes=VMEM_LIMIT),
        cost_estimate=cost(PIECE_COST),
        name="weight_piece",
    )(dh, *blocks, *before)


def total_kernel(part_ref, twin_ref, *refs):
    rows = part_ref.shape[0] // 2
    for here, there in ((pl.ds(0, rows), pl.ds(rows, rows)), (pl.ds(rows, rows), pl.ds(0, rows))):
        total = part_ref[here, :].astype(jnp.float32) + twin_ref[there, :].astype(jnp.float32)
        for ref in refs[:-1]:
            total = total + ref[here, :].astype(jnp.float32)
        refs[-1][here, :] = total.astype(refs[-1].dtype)


def total(*terms):
    return pl.pallas_call(
        total_kernel,
        out_shape=jax.ShapeDtypeStruct(terms[0].shape, terms[0].dtype),
        in_specs=[WHOLE] * len(terms),
        out_specs=WHOLE,
        compiler_params=pltpu.CompilerParams(vmem_limit_bytes=VMEM_LIMIT),
        cost_estimate=cost(0.1),
        name="total",
    )(*terms)


def halves_kernel(own_ref, came_ref, kept_ref, sent_ref):
    rows = kept_ref.shape[0]
    for ref, here in ((kept_ref, pl.ds(0, rows)), (sent_ref, pl.ds(rows, rows))):
        both = own_ref[here, :].astype(jnp.float32) + came_ref[here, :].astype(jnp.float32)
        ref[...] = both.astype(ref.dtype)


def halves(own, came):
    shape = (own.shape[0] // 2, own.shape[1])
    return pl.pallas_call(
        halves_kernel,
        out_shape=(
            jax.ShapeDtypeStruct(shape, jnp.float32),
            jax.ShapeDtypeStruct(shape, jnp.bfloat16),
        ),
        in_specs=[WHOLE, WHOLE],
        out_specs=(WHOLE, WHOLE),
        compiler_params=pltpu.CompilerParams(vmem_limit_bytes=VMEM_LIMIT),
        cost_estimate=cost(0.1),
        name="halves",
    )(own, came)


def last_kernel(me_ref, mine_ref, mine_came_ref, other_ref, other_came_ref, out_ref):
    core = me_ref[0] % 2
    half = mine_ref.shape[1]
    pairs = ((core, mine_ref, mine_came_ref), (1 - core, other_ref, other_came_ref))
    for number, kept, came in pairs:
        here = pl.ds(pl.multiple_of(number * half, half), half)
        out_ref[:, here] = (kept[...] + came[...].astype(jnp.float32)).astype(out_ref.dtype)


def last(me, mine, mine_came, other, other_came):
    shape = (mine.shape[0], 2 * mine.shape[1])
    return pl.pallas_call(
        last_kernel,
        out_shape=jax.ShapeDtypeStruct(shape, jnp.bfloat16),
        in_specs=[SCALAR] + [WHOLE] * 4,
        out_specs=WHOLE,
        compiler_params=pltpu.CompilerParams(vmem_limit_bytes=VMEM_LIMIT),
        cost_estimate=cost(0.3),
        name="last",
    )(me, mine, mine_came, other, other_came)


def after(x, *others):
    return lax.optimization_barrier((x, *others))[0]


def on_device(out_grad, pre_act, layer_input, weight):
    n = lax.axis_size("gx")
    rows, width = layer_input.shape
    if n != 2 * RING or rows % 16 or width % (2 * PIECES * PIECE_STEPS * 128):
        return plain(out_grad, pre_act, layer_input, weight)

    along, across = ring_pairs()
    twins = [(i, i ^ 1) for i in range(n)]

    def ring(x):
        return lax.ppermute(x, "gx", along)

    def swap(x):
        return lax.ppermute(x, "gx", twins)

    out_grad, pre_act, weight = (
        pltpu.with_memory_space_constraint(x, pltpu.HBM) for x in (out_grad, pre_act, weight)
    )
    me = lax.axis_index("gx").astype(jnp.int32).reshape(1)

    a1, twin = ring(layer_input), swap(layer_input)
    dh, dht, w = hidden(me, out_grad, pre_act, weight)
    b1 = lax.ppermute(after(layer_input, dh), "gx", across)

    def product(other, piece, w, before, *ties):
        return input_piece(me, after(dht, *ties), w, weight, before, other, piece)

    go, w = product(True, 0, w, ())
    a1 = after(a1, go[0])
    a2, sa1 = ring(a1), swap(a1)
    go, w = product(True, 1, w, go, a1, twin)
    b1 = after(b1, go[0])
    b2, sb1 = ring(b1), swap(b1)
    go, w = product(True, 2, w, go, b1, sa1)
    a2 = after(a2, go[0])
    a3, sa2 = ring(a2), swap(a2)
    go, w = product(True, 3, w, go, a2, sb1)
    b2 = after(b2, go[0])
    b3, sb2 = ring(b2), swap(b2)
    gm, w = product(False, 0, w, (), b2, sa2)
    a3 = after(a3, gm[0])
    a4, sa3 = ring(a3), swap(a3)
    own_o, behind_o, opposite_o, ahead_o = go[0], go[1:4], go[4], go[5:]
    opposite_from = swap(after(opposite_o, gm[0]))
    gm, w = product(False, 1, w, gm, a3, sb2)
    gm, w = product(False, 2, w, gm, sa3)
    gm, _ = product(False, 3, w, gm, b3, opposite_from)
    own_m, behind_m, opposite_m, ahead_m = gm[0], gm[1:4], gm[4], gm[5:]
    sent = total(opposite_m, opposite_from)
    r4m = ring(sent)
    a4 = after(a4, sent)
    sa4 = swap(a4)
    from_o, from_m = [None] * 3, [None] * 3
    from_o[2], from_m[2] = swap(after(behind_m[2], sent)), swap(after(behind_o[2], sent))

    def gradient(piece, before, *ties):
        before = before[::-1]
        return weight_piece(after(dh, *ties), blocks, before, piece)

    def send(k, ahead, came, *ring_terms):
        return total(ahead[k - 1], came[k - 1], *ring_terms)

    sb3 = swap(after(b3, sent))
    blocks = (layer_input, twin, a1, b1, a2, b2, a3, b3, a4, sa4, sb1, sa1, sb2, sa2, sb3, sa3)
    gw = gradient(0, (), sent, from_o[2])
    from_o[2] = after(from_o[2], gw[1])
    sent = send(3, ahead_o, from_o)
    r3o = ring(sent)
    gw = gradient(1, gw, sent)
    sent = send(3, ahead_m, from_m, after(r4m, gw[1]))
    r3m = ring(sent)
    from_o[1], from_m[1] = swap(after(behind_m[1], sent)), swap(after(behind_o[1], sent))
    gw = gradient(2, gw, sent)
    sent = send(2, ahead_o, from_o, after(r3o, gw[1]))
    r2o = ring(sent)
    from_o[0], from_m[0] = swap(after(behind_m[0], sent)), swap(after(behind_o[0], sent))
    gw = gradient(3, gw, sent, from_m[1])
    sent = send(2, ahead_m, from_m, after(r3m, gw[1]))
    r2m = ring(sent)
    gw = gradient(4, gw, sent, from_o[0], from_m[0])
    sent = send(1, ahead_o, from_o, after(r2o, gw[1]))
    r1o = ring(sent)
    gw = gradient(5, gw, sent)
    sent = send(1, ahead_m, from_m, after(r2m, gw[1]))
    r1m = ring(sent)
    gw = gradient(6, gw, sent)
    kept_o, sent_o = halves(own_o, after(r1o, gw[1]))
    came_m = swap(sent_o)
    gw = gradient(7, gw, sent_o)
    kept_m, sent_m = halves(own_m, after(r1m, gw[0]))
    came_o = swap(sent_m)
    return (last(me, kept_m, came_m, kept_o, came_o), gw[0])


def solution(mesh):
    placed = (P("group", "gx"), P("group", "gx"), P(("group", "gx"), None), P(None, "gx"))
    return jax.shard_map(
        on_device,
        mesh=mesh,
        in_specs=placed,
        out_specs=(P(("group", "gx"), None), P(None, ("group", "gx"))),
        check_vma=False,
    )
```

```python
import math

import jax
import jax.numpy as jnp
from jax import lax
from jax.experimental import pallas as pl
from jax.experimental.pallas import tpu as pltpu
from jax.sharding import PartitionSpec as P

RING = 8
PIECE_STEPS = 2
PIECE_COST = 0.1
PIECES = 4
VMEM_LIMIT = 16 * 1024 * 1024
WHOLE = pl.BlockSpec(memory_space=pltpu.VMEM)
OUTSIDE = pl.BlockSpec(memory_space=pltpu.HBM)


def cost(microseconds):
    return pl.CostEstimate(
        flops=int(microseconds * 1.15e9), bytes_accessed=0, transcendentals=0
    )


ANYWHERE = pl.BlockSpec(memory_space=pl.ANY)
SCALAR = pl.BlockSpec(memory_space=pltpu.SMEM)


def gelu_slope(pre):
    coeff = math.sqrt(2.0 / math.pi)
    square = pre * pre
    tanh_value = jnp.tanh(pre * (coeff + coeff * 0.044715 * square))
    inner_slope = coeff + 3.0 * 0.044715 * coeff * square
    return (0.5 + 0.5 * tanh_value) * (1.0 + pre * (1.0 - tanh_value) * inner_slope)


def plain(out_grad, pre_act, layer_input, weight):
    slope = gelu_slope(pre_act.astype(jnp.float32))
    grad_hidden = (out_grad.astype(jnp.float32) * slope).astype(jnp.bfloat16)
    local_grad = lax.dot_general(
        lax.all_gather(layer_input, "gx", axis=0, tiled=True),
        grad_hidden,
        (((0,), (0,)), ((), ())),
        preferred_element_type=jnp.float32,
    )
    grad_input = lax.psum_scatter(
        lax.dot_general(
            grad_hidden, weight, (((1,), (1,)), ((), ())), preferred_element_type=jnp.float32
        ),
        "gx",
        scatter_dimension=0,
        tiled=True,
    ).astype(jnp.bfloat16)
    return (grad_input, local_grad.astype(jnp.bfloat16))


def chip_at(place):
    place = place & (RING - 1)
    return jnp.where(place < RING // 2, 2 * place, 2 * (RING - 1 - place) + 1)


def place_of(chip):
    return jnp.where(chip % 2 == 0, chip // 2, RING - 1 - chip // 2)


def ring_pairs():
    path = [2 * p if p < RING // 2 else 2 * (RING - 1 - p) + 1 for p in range(RING)]
    along, gather_across, sum_across = [], [], []
    for place, chip in enumerate(path):
        ahead, behind = path[(place + 1) % RING], path[(place - 1) % RING]
        along += [(2 * chip, 2 * ahead), (2 * chip + 1, 2 * behind + 1)]
        gather_across += [(2 * chip, 2 * behind + 1), (2 * chip + 1, 2 * ahead)]
        sum_across += [(2 * chip, 2 * ahead + 1), (2 * chip + 1, 2 * behind)]
    return along, gather_across, sum_across


def chip_order(me):
    way = jnp.where(me % 2 == 0, 1, -1)
    place = place_of(me // 2)
    steps = [0, -1, -2, -3, 4, 1, 2, 3]
    return [chip_at(place + way * s + RING) for s in steps]


def hidden_kernel(me_ref, og_hbm, pre_hbm, w_hbm, dh_ref, dht_ref, w_ref, og_ref, pre_ref, sems):
    rows = dh_ref.shape[0] // (2 * RING)
    me = me_ref[0]
    copies = []
    for i, chip in enumerate(chip_order(me)):
        for j, core in enumerate((me % 2, 1 - me % 2)):
            source = pl.ds(pl.multiple_of((2 * chip + core) * rows, rows), rows)
            block = pl.ds((2 * i + j) * rows, rows)
            for k, (hbm, ref) in enumerate(((og_hbm, og_ref), (pre_hbm, pre_ref))):
                copy = pltpu.make_async_copy(
                    hbm.at[source, :], ref.at[block, :], sems.at[k, 2 * i + j]
                )
                copy.start()
                copies.append(copy)
    wide = w_ref.shape[0]
    first = first_row(me_ref, True, 0, w_hbm.shape[0] // 2, wide)
    fetch = pltpu.make_async_copy(w_hbm.at[pl.ds(first, wide), :], w_ref, sems.at[2, 0])
    fetch.start()
    for i in range(RING // 2):
        for copy in copies[8 * i : 8 * (i + 1)]:
            copy.wait()
        block = pl.ds(4 * i * rows, 4 * rows)
        pre = pre_ref[block, :].astype(jnp.float32)
        og = og_ref[block, :].astype(jnp.float32)
        dh = (og * gelu_slope(pre)).astype(jnp.bfloat16)
        dh_ref[block, :] = dh
        dht_ref[:, block] = dh.T
    fetch.wait()


def hidden(me, out_grad, pre_act, weight):
    shape, dtype = out_grad.shape, out_grad.dtype
    return pl.pallas_call(
        hidden_kernel,
        out_shape=(
            jax.ShapeDtypeStruct(shape, dtype),
            jax.ShapeDtypeStruct(shape[::-1], dtype),
            jax.ShapeDtypeStruct((weight.shape[0] // (2 * PIECES), shape[1]), dtype),
        ),
        in_specs=[SCALAR, OUTSIDE, OUTSIDE, OUTSIDE],
        out_specs=(WHOLE, WHOLE, WHOLE),
        scratch_shapes=[
            pltpu.VMEM(shape, dtype),
            pltpu.VMEM(shape, dtype),
            pltpu.SemaphoreType.DMA((3, 2 * RING)),
        ],
        compiler_params=pltpu.CompilerParams(vmem_limit_bytes=VMEM_LIMIT),
        cost_estimate=cost(1),
        name="hidden",
    )(me, out_grad, pre_act, weight)


def first_row(me_ref, other, piece, half, wide):
    core = me_ref[0] % 2
    number = 1 - core if other else core
    return pl.multiple_of(number * half + piece * wide, wide)


def input_kernel(me_ref, dht_ref, w_ref, w_hbm, *refs, other, piece, wide, more):
    outs, part_ref, sems = refs[-(RING + 3 + more) :][: RING + 1], refs[-2], refs[-1]
    half = outs[0].shape[1]
    if more:
        following = (other, piece + 1) if piece + 1 < PIECES else (False, 0)
        fetch = pltpu.make_async_copy(
            w_hbm.at[pl.ds(first_row(me_ref, *following, half, wide), wide), :],
            refs[-3],
            sems.at[PIECE_STEPS, 0],
        )
        fetch.start()
    steps = PIECE_STEPS if other else 1
    step = wide // steps
    stores = []
    for i in range(steps):
        here = pl.ds(i * step, step)
        part = jnp.dot(w_ref[here, :], dht_ref[...], preferred_element_type=jnp.float32)
        part_ref[:, here] = part.astype(jnp.bfloat16).T
        at = 0
        for j, out in enumerate(outs):
            rows = out.shape[0]
            store = pltpu.make_async_copy(
                part_ref.at[pl.ds(at, rows), here],
                out.at[:, pl.ds(piece * wide + i * step, step)],
                sems.at[i, j],
            )
            store.start()
            stores.append(store)
            at += rows
    for store in stores:
        store.wait()
    if more:
        fetch.wait()


def input_piece(me, dht, w, weight, before, other, piece):
    ff, tokens = dht.shape
    half = weight.shape[0] // 2
    wide = half // PIECES
    rows = tokens // RING
    more = other or piece + 1 < PIECES
    outs = tuple(
        jax.ShapeDtypeStruct((count, half), jnp.bfloat16)
        for count in [rows // 2] * 2 + [rows] * (RING - 1)
    )
    following = (jax.ShapeDtypeStruct((wide, ff), jnp.bfloat16),) if more else ()
    result = pl.pallas_call(
        lambda *refs: input_kernel(*refs, other=other, piece=piece, wide=wide, more=more),
        out_shape=outs + following,
        in_specs=[SCALAR, WHOLE, WHOLE, OUTSIDE] + [ANYWHERE] * len(before),
        out_specs=(ANYWHERE,) * len(outs) + (WHOLE,) * len(following),
        input_output_aliases={4 + i: i for i in range(len(before))},
        scratch_shapes=[
            pltpu.VMEM((tokens, wide), jnp.bfloat16),
            pltpu.SemaphoreType.DMA((PIECE_STEPS + 1, len(outs))),
        ],
        compiler_params=pltpu.CompilerParams(vmem_limit_bytes=VMEM_LIMIT),
        cost_estimate=cost(PIECE_COST),
        name="input_piece",
    )(me, dht, w, weight, *before)
    return result[: len(outs)], (result[-1] if more else None)


def weight_kernel(dh_ref, *refs, piece, wide, step):
    blocks, refs = refs[: 2 * RING], refs[2 * RING :]
    out_hbm, stage, sems = refs[-3:]
    width, columns = out_hbm.shape
    copies = []

    def store(source, number, i):
        here = pl.ds(i * step, step)
        rows = pl.ds(number * wide, wide)
        copy = pltpu.make_async_copy(
            source.at[:, here], out_hbm.at[rows, here], sems.at[piece - number, i]
        )
        copy.start()
        copies.append(copy)

    if piece:
        for i in range(columns // step):
            store(refs[0], piece - 1, i)
    x = jnp.concatenate([b[:, pl.ds(piece * wide, wide)] for b in blocks], axis=0).T
    for i in range(columns // step):
        here = pl.ds(i * step, step)
        stage[:, here] = jnp.dot(
            x, dh_ref[:, here], preferred_element_type=jnp.float32
        ).astype(jnp.bfloat16)
        if (piece + 1) * wide == width:
            store(stage, piece, i)
    for copy in copies:
        copy.wait()


def weight_piece(dh, blocks, before, piece):
    tokens, ff = dh.shape
    width = blocks[0].shape[1]
    wide = width // (2 * PIECES)
    step = 512 if ff % 512 == 0 else 128
    ends = piece == 2 * PIECES - 1
    stage = jax.ShapeDtypeStruct((wide, ff), jnp.bfloat16)
    return pl.pallas_call(
        lambda *refs: weight_kernel(*refs, piece=piece, wide=wide, step=step),
        out_shape=(jax.ShapeDtypeStruct((width, ff), jnp.bfloat16),) + (stage,) * (not ends),
        in_specs=[WHOLE] * (1 + 2 * RING) + ([WHOLE, OUTSIDE] if before else []),
        out_specs=(OUTSIDE,) + (WHOLE,) * (not ends),
        input_output_aliases={2 + 2 * RING: 0} if before else {},
        scratch_shapes=[pltpu.VMEM(stage.shape, stage.dtype)] * ends
        + [pltpu.SemaphoreType.DMA((2, ff // step))],
        compiler_params=pltpu.CompilerParams(vmem_limit_bytes=VMEM_LIMIT),
        cost_estimate=cost(PIECE_COST),
        name="weight_piece",
    )(dh, *blocks, *before)


def total_kernel(part_ref, twin_ref, *refs, count):
    rows = part_ref.shape[0] // 2
    came, outs = refs[:-count], refs[-count:]
    for i in range(2):
        here, there = pl.ds(i * rows, rows), pl.ds((1 - i) * rows, rows)
        sums = part_ref[here, :].astype(jnp.float32) + twin_ref[there, :].astype(jnp.float32)
        for ref in came:
            sums = sums + ref[here, :].astype(jnp.float32)
        if count == 1:
            outs[0][here, :] = sums.astype(outs[0].dtype)
        else:
            outs[i][...] = sums.astype(outs[i].dtype)


def total(*terms, count=1):
    rows, half = terms[0].shape
    out = jax.ShapeDtypeStruct((rows // count, half), terms[0].dtype)
    result = pl.pallas_call(
        lambda *refs: total_kernel(*refs, count=count),
        out_shape=(out,) * count,
        in_specs=[WHOLE] * len(terms),
        out_specs=(WHOLE,) * count,
        compiler_params=pltpu.CompilerParams(vmem_limit_bytes=VMEM_LIMIT),
        cost_estimate=cost(0.1),
        name="total",
    )(*terms)
    return result[0] if count == 1 else result


def last_kernel(me_ref, *refs):
    out_ref = refs[-1]
    core = me_ref[0] % 2
    half = refs[0].shape[1]
    count = (len(refs) - 1) // 2
    for number, terms in ((core, refs[:count]), (1 - core, refs[count:-1])):
        sums = terms[0][...].astype(jnp.float32)
        for term in terms[1:]:
            sums = sums + term[...].astype(jnp.float32)
        here = pl.ds(pl.multiple_of(number * half, half), half)
        out_ref[:, here] = sums.astype(out_ref.dtype)


def last(me, mine, other):
    rows, half = mine[0].shape
    return pl.pallas_call(
        last_kernel,
        out_shape=jax.ShapeDtypeStruct((rows, 2 * half), jnp.bfloat16),
        in_specs=[SCALAR] + [WHOLE] * (len(mine) + len(other)),
        out_specs=WHOLE,
        compiler_params=pltpu.CompilerParams(vmem_limit_bytes=VMEM_LIMIT),
        cost_estimate=cost(0.3),
        name="last",
    )(me, *mine, *other)


def after(x, *others):
    return lax.optimization_barrier((x, *others))[0]


def on_device(out_grad, pre_act, layer_input, weight):
    n = lax.axis_size("gx")
    rows, width = layer_input.shape
    if n != 2 * RING or rows % 16 or width % (2 * PIECES * PIECE_STEPS * 128):
        return plain(out_grad, pre_act, layer_input, weight)

    along, gather_across, sum_across = ring_pairs()
    twins = [(i, i ^ 1) for i in range(n)]

    def ring(x):
        return lax.ppermute(x, "gx", along)

    def swap(x):
        return lax.ppermute(x, "gx", twins)

    out_grad, pre_act, weight = (
        pltpu.with_memory_space_constraint(x, pltpu.HBM) for x in (out_grad, pre_act, weight)
    )
    me = lax.axis_index("gx").astype(jnp.int32).reshape(1)

    dh, dht, w = hidden(me, out_grad, pre_act, weight)
    a1, twin = ring(after(layer_input, dh)), swap(layer_input)

    def product(other, piece, w, before, *ties):
        return input_piece(me, after(dht, *ties), w, weight, before, other, piece)

    go, w = product(True, 0, w, ())
    b1 = lax.ppermute(after(layer_input, go[0]), "gx", gather_across)
    go, w = product(True, 1, w, go)
    a1 = after(a1, go[0])
    a2, sa1 = ring(a1), swap(a1)
    go, w = product(True, 2, w, go, a1, twin)
    b1 = after(b1, go[0])
    b2, sb1 = ring(b1), swap(b1)
    go, w = product(True, 3, w, go, b1, sa1)
    a2 = after(a2, go[0])
    a3, sa2 = ring(a2), swap(a2)
    gm, w = product(False, 0, w, (), a2, sb1)
    b2 = after(b2, gm[0])
    b3, sb2 = ring(b2), swap(b2)
    gm, w = product(False, 1, w, gm, b2, sa2)
    a3 = after(a3, gm[0])
    a4, sa3 = ring(a3), swap(a3)
    own_o, behind_o, opposite_o, ahead_o = go[:2], go[2:5], go[5], go[6:]
    opposite_from = swap(after(opposite_o, gm[0]))
    gm, w = product(False, 2, w, gm, a3, sb2)
    gm, _ = product(False, 3, w, gm, sa3, b3, opposite_from)
    own_m, behind_m, opposite_m, ahead_m = gm[:2], gm[2:5], gm[5], gm[6:]
    sent = total(opposite_m, opposite_from)
    r4m = ring(sent)
    a4, b3 = after(a4, sent), after(b3, sent)
    sa4, sb3 = swap(a4), swap(b3)
    from_o, from_m = [None] * 3, [None] * 3
    from_o[2], from_m[2] = swap(after(behind_m[2], sent)), swap(after(behind_o[2], sent))

    def gradient(piece, before, *ties):
        before = before[::-1]
        return weight_piece(after(dh, *ties), blocks, before, piece)

    def send(k, ahead, came, *ring_terms):
        return total(ahead[k - 1], came[k - 1], *ring_terms)

    blocks = (layer_input, twin, a1, b1, a2, b2, a3, b3, a4, sa4, sb1, sa1, sb2, sa2, sb3, sa3)
    gw = gradient(0, (), sent, from_o[2])
    from_o[2] = after(from_o[2], gw[1])
    sent = send(3, ahead_o, from_o)
    r3o = ring(sent)
    gw = gradient(1, gw, sent)
    sent = send(3, ahead_m, from_m, after(r4m, gw[1]))
    r3m = ring(sent)
    from_o[1], from_m[1] = swap(after(behind_m[1], sent)), swap(after(behind_o[1], sent))
    gw = gradient(2, gw, sent)
    sent = send(2, ahead_o, from_o, after(r3o, gw[1]))
    r2o = ring(sent)
    from_o[0], from_m[0] = swap(after(behind_m[0], sent)), swap(after(behind_o[0], sent))
    gw = gradient(3, gw, sent, from_m[1])
    sent = send(2, ahead_m, from_m, after(r3m, gw[1]))
    r2m = ring(sent)
    gw = gradient(4, gw, sent, from_o[0], from_m[0])
    sent = total(ahead_o[0], from_o[0], after(r2o, gw[1]), count=2)
    r1o, x1m = ring(sent[0]), lax.ppermute(sent[1], "gx", sum_across)
    own_from_m, own_from_o = swap(after(own_o[1], sent[0])), swap(after(own_m[1], sent[0]))
    gw = gradient(5, gw, sent[0])
    sent = total(ahead_m[0], from_m[0], after(r2m, gw[1]), count=2)
    r1m, x1o = ring(sent[0]), lax.ppermute(sent[1], "gx", sum_across)
    gw = gradient(6, gw, sent[0])
    gw = gradient(7, gw, own_from_m, own_from_o)
    r1m = after(r1m, gw[0])
    mine = (own_m[0], own_from_m, r1m, x1m)
    return (last(me, mine, (own_o[0], own_from_o, r1o, x1o)), gw[0])


def solution(mesh):
    placed = (P("group", "gx"), P("group", "gx"), P(("group", "gx"), None), P(None, "gx"))
    return jax.shard_map(
        on_device,
        mesh=mesh,
        in_specs=placed,
        out_specs=(P(("group", "gx"), None), P(None, ("group", "gx"))),
        check_vma=False,
    )
```

```python
import math

import jax
import jax.numpy as jnp
from jax import lax
from jax.experimental import pallas as pl
from jax.experimental.pallas import tpu as pltpu
from jax.sharding import PartitionSpec as P

RING = 8
PIECE_STEPS = 2
PIECE_COST = 0.1
PIECES = 4
VMEM_LIMIT = 16 * 1024 * 1024
WHOLE = pl.BlockSpec(memory_space=pltpu.VMEM)
OUTSIDE = pl.BlockSpec(memory_space=pltpu.HBM)


def cost(microseconds):
    return pl.CostEstimate(
        flops=int(microseconds * 1.15e9), bytes_accessed=0, transcendentals=0
    )


ANYWHERE = pl.BlockSpec(memory_space=pl.ANY)
SCALAR = pl.BlockSpec(memory_space=pltpu.SMEM)


def gelu_slope(pre):
    coeff = math.sqrt(2.0 / math.pi)
    square = pre * pre
    tanh_value = jnp.tanh(pre * (coeff + coeff * 0.044715 * square))
    inner_slope = coeff + 3.0 * 0.044715 * coeff * square
    return (0.5 + 0.5 * tanh_value) * (1.0 + pre * (1.0 - tanh_value) * inner_slope)


def plain(out_grad, pre_act, layer_input, weight):
    slope = gelu_slope(pre_act.astype(jnp.float32))
    grad_hidden = (out_grad.astype(jnp.float32) * slope).astype(jnp.bfloat16)
    local_grad = lax.dot_general(
        lax.all_gather(layer_input, "gx", axis=0, tiled=True),
        grad_hidden,
        (((0,), (0,)), ((), ())),
        preferred_element_type=jnp.float32,
    )
    grad_input = lax.psum_scatter(
        lax.dot_general(
            grad_hidden, weight, (((1,), (1,)), ((), ())), preferred_element_type=jnp.float32
        ),
        "gx",
        scatter_dimension=0,
        tiled=True,
    ).astype(jnp.bfloat16)
    return (grad_input, local_grad.astype(jnp.bfloat16))


def chip_at(place):
    place = place & (RING - 1)
    return jnp.where(place < RING // 2, 2 * place, 2 * (RING - 1 - place) + 1)


def place_of(chip):
    return jnp.where(chip % 2 == 0, chip // 2, RING - 1 - chip // 2)


def ring_pairs():
    path = [2 * p if p < RING // 2 else 2 * (RING - 1 - p) + 1 for p in range(RING)]
    along, across = [], []
    for place, chip in enumerate(path):
        ahead, behind = path[(place + 1) % RING], path[(place - 1) % RING]
        along += [(2 * chip, 2 * ahead), (2 * chip + 1, 2 * behind + 1)]
        across += [(2 * chip, 2 * behind + 1), (2 * chip + 1, 2 * ahead)]
    return along, across


def chip_order(me):
    way = jnp.where(me % 2 == 0, 1, -1)
    place = place_of(me // 2)
    steps = [0, -1, -2, -3, 4, 1, 2, 3]
    return [chip_at(place + way * s + RING) for s in steps]


def hidden_kernel(me_ref, og_hbm, pre_hbm, w_hbm, dh_ref, dht_ref, w_ref, og_ref, pre_ref, sems):
    rows = dh_ref.shape[0] // (2 * RING)
    me = me_ref[0]
    copies = []
    for i, chip in enumerate(chip_order(me)):
        for j, core in enumerate((me % 2, 1 - me % 2)):
            source = pl.ds(pl.multiple_of((2 * chip + core) * rows, rows), rows)
            block = pl.ds((2 * i + j) * rows, rows)
            for k, (hbm, ref) in enumerate(((og_hbm, og_ref), (pre_hbm, pre_ref))):
                copy = pltpu.make_async_copy(
                    hbm.at[source, :], ref.at[block, :], sems.at[k, 2 * i + j]
                )
                copy.start()
                copies.append(copy)
    wide = w_ref.shape[0]
    first = first_row(me_ref, True, 0, w_hbm.shape[0] // 2, wide)
    fetch = pltpu.make_async_copy(w_hbm.at[pl.ds(first, wide), :], w_ref, sems.at[2, 0])
    fetch.start()
    for i in range(RING // 2):
        for copy in copies[8 * i : 8 * (i + 1)]:
            copy.wait()
        block = pl.ds(4 * i * rows, 4 * rows)
        pre = pre_ref[block, :].astype(jnp.float32)
        og = og_ref[block, :].astype(jnp.float32)
        dh = (og * gelu_slope(pre)).astype(jnp.bfloat16)
        dh_ref[block, :] = dh
        dht_ref[:, block] = dh.T
    fetch.wait()


def hidden(me, out_grad, pre_act, weight):
    shape, dtype = out_grad.shape, out_grad.dtype
    return pl.pallas_call(
        hidden_kernel,
        out_shape=(
            jax.ShapeDtypeStruct(shape, dtype),
            jax.ShapeDtypeStruct(shape[::-1], dtype),
            jax.ShapeDtypeStruct((weight.shape[0] // (2 * PIECES), shape[1]), dtype),
        ),
        in_specs=[SCALAR, OUTSIDE, OUTSIDE, OUTSIDE],
        out_specs=(WHOLE, WHOLE, WHOLE),
        scratch_shapes=[
            pltpu.VMEM(shape, dtype),
            pltpu.VMEM(shape, dtype),
            pltpu.SemaphoreType.DMA((3, 2 * RING)),
        ],
        compiler_params=pltpu.CompilerParams(vmem_limit_bytes=VMEM_LIMIT),
        cost_estimate=cost(1),
        name="hidden",
    )(me, out_grad, pre_act, weight)


def first_row(me_ref, other, piece, half, wide):
    core = me_ref[0] % 2
    number = 1 - core if other else core
    return pl.multiple_of(number * half + piece * wide, wide)


def input_kernel(me_ref, dht_ref, w_ref, w_hbm, *refs, other, piece, wide, more):
    outs, part_ref, sems = refs[-(RING + 2 + more) :][:RING], refs[-2], refs[-1]
    half = outs[0].shape[1]
    if more:
        following = (other, piece + 1) if piece + 1 < PIECES else (False, 0)
        fetch = pltpu.make_async_copy(
            w_hbm.at[pl.ds(first_row(me_ref, *following, half, wide), wide), :],
            refs[-3],
            sems.at[PIECE_STEPS, 0],
        )
        fetch.start()
    steps = PIECE_STEPS if other else 1
    step = wide // steps
    stores = []
    for i in range(steps):
        here = pl.ds(i * step, step)
        part = jnp.dot(w_ref[here, :], dht_ref[...], preferred_element_type=jnp.float32)
        part_ref[:, here] = part.astype(jnp.bfloat16).T
        for j, out in enumerate(outs):
            rows = out.shape[0]
            store = pltpu.make_async_copy(
                part_ref.at[pl.ds(j * rows, rows), here],
                out.at[:, pl.ds(piece * wide + i * step, step)],
                sems.at[i, j],
            )
            store.start()
            stores.append(store)
    for store in stores:
        store.wait()
    if more:
        fetch.wait()


def input_piece(me, dht, w, weight, before, other, piece):
    ff, tokens = dht.shape
    half = weight.shape[0] // 2
    wide = half // PIECES
    rows = tokens // RING
    more = other or piece + 1 < PIECES
    outs = (jax.ShapeDtypeStruct((rows, half), jnp.bfloat16),) * RING
    following = (jax.ShapeDtypeStruct((wide, ff), jnp.bfloat16),) if more else ()
    result = pl.pallas_call(
        lambda *refs: input_kernel(*refs, other=other, piece=piece, wide=wide, more=more),
        out_shape=outs + following,
        in_specs=[SCALAR, WHOLE, WHOLE, OUTSIDE] + [ANYWHERE] * len(before),
        out_specs=(ANYWHERE,) * RING + (WHOLE,) * len(following),
        input_output_aliases={4 + i: i for i in range(len(before))},
        scratch_shapes=[
            pltpu.VMEM((tokens, wide), jnp.bfloat16),
            pltpu.SemaphoreType.DMA((PIECE_STEPS + 1, RING)),
        ],
        compiler_params=pltpu.CompilerParams(vmem_limit_bytes=VMEM_LIMIT),
        cost_estimate=cost(PIECE_COST),
        name="input_piece",
    )(me, dht, w, weight, *before)
    return result[:RING], (result[RING] if more else None)


def weight_kernel(dh_ref, *refs, piece, wide, step):
    blocks, refs = refs[: 2 * RING], refs[2 * RING :]
    out_hbm, stage, sems = refs[-3:]
    width, columns = out_hbm.shape
    copies = []

    def store(source, number, i):
        here = pl.ds(i * step, step)
        rows = pl.ds(number * wide, wide)
        copy = pltpu.make_async_copy(
            source.at[:, here], out_hbm.at[rows, here], sems.at[piece - number, i]
        )
        copy.start()
        copies.append(copy)

    if piece:
        for i in range(columns // step):
            store(refs[0], piece - 1, i)
    x = jnp.concatenate([b[:, pl.ds(piece * wide, wide)] for b in blocks], axis=0).T
    for i in range(columns // step):
        here = pl.ds(i * step, step)
        stage[:, here] = jnp.dot(
            x, dh_ref[:, here], preferred_element_type=jnp.float32
        ).astype(jnp.bfloat16)
        if (piece + 1) * wide == width:
            store(stage, piece, i)
    for copy in copies:
        copy.wait()


def weight_piece(dh, blocks, before, piece):
    tokens, ff = dh.shape
    width = blocks[0].shape[1]
    wide = width // (2 * PIECES)
    step = 512 if ff % 512 == 0 else 128
    ends = piece == 2 * PIECES - 1
    stage = jax.ShapeDtypeStruct((wide, ff), jnp.bfloat16)
    return pl.pallas_call(
        lambda *refs: weight_kernel(*refs, piece=piece, wide=wide, step=step),
        out_shape=(jax.ShapeDtypeStruct((width, ff), jnp.bfloat16),) + (stage,) * (not ends),
        in_specs=[WHOLE] * (1 + 2 * RING) + ([WHOLE, OUTSIDE] if before else []),
        out_specs=(OUTSIDE,) + (WHOLE,) * (not ends),
        input_output_aliases={2 + 2 * RING: 0} if before else {},
        scratch_shapes=[pltpu.VMEM(stage.shape, stage.dtype)] * ends
        + [pltpu.SemaphoreType.DMA((2, ff // step))],
        compiler_params=pltpu.CompilerParams(vmem_limit_bytes=VMEM_LIMIT),
        cost_estimate=cost(PIECE_COST),
        name="weight_piece",
    )(dh, *blocks, *before)


def total_kernel(part_ref, twin_ref, *refs):
    rows = part_ref.shape[0] // 2
    for here, there in ((pl.ds(0, rows), pl.ds(rows, rows)), (pl.ds(rows, rows), pl.ds(0, rows))):
        total = part_ref[here, :].astype(jnp.float32) + twin_ref[there, :].astype(jnp.float32)
        for ref in refs[:-1]:
            total = total + ref[here, :].astype(jnp.float32)
        refs[-1][here, :] = total.astype(refs[-1].dtype)


def total(*terms):
    return pl.pallas_call(
        total_kernel,
        out_shape=jax.ShapeDtypeStruct(terms[0].shape, terms[0].dtype),
        in_specs=[WHOLE] * len(terms),
        out_specs=WHOLE,
        compiler_params=pltpu.CompilerParams(vmem_limit_bytes=VMEM_LIMIT),
        cost_estimate=cost(0.1),
        name="total",
    )(*terms)


def halves_kernel(own_ref, came_ref, kept_ref, sent_ref):
    rows = kept_ref.shape[0]
    for ref, here in ((kept_ref, pl.ds(0, rows)), (sent_ref, pl.ds(rows, rows))):
        both = own_ref[here, :].astype(jnp.float32) + came_ref[here, :].astype(jnp.float32)
        ref[...] = both.astype(ref.dtype)


def halves(own, came):
    shape = (own.shape[0] // 2, own.shape[1])
    return pl.pallas_call(
        halves_kernel,
        out_shape=(
            jax.ShapeDtypeStruct(shape, jnp.float32),
            jax.ShapeDtypeStruct(shape, jnp.bfloat16),
        ),
        in_specs=[WHOLE, WHOLE],
        out_specs=(WHOLE, WHOLE),
        compiler_params=pltpu.CompilerParams(vmem_limit_bytes=VMEM_LIMIT),
        cost_estimate=cost(0.1),
        name="halves",
    )(own, came)


def last_kernel(me_ref, mine_ref, mine_came_ref, other_ref, other_came_ref, out_ref):
    core = me_ref[0] % 2
    half = mine_ref.shape[1]
    pairs = ((core, mine_ref, mine_came_ref), (1 - core, other_ref, other_came_ref))
    for number, kept, came in pairs:
        here = pl.ds(pl.multiple_of(number * half, half), half)
        out_ref[:, here] = (kept[...] + came[...].astype(jnp.float32)).astype(out_ref.dtype)


def last(me, mine, mine_came, other, other_came):
    shape = (mine.shape[0], 2 * mine.shape[1])
    return pl.pallas_call(
        last_kernel,
        out_shape=jax.ShapeDtypeStruct(shape, jnp.bfloat16),
        in_specs=[SCALAR] + [WHOLE] * 4,
        out_specs=WHOLE,
        compiler_params=pltpu.CompilerParams(vmem_limit_bytes=VMEM_LIMIT),
        cost_estimate=cost(0.3),
        name="last",
    )(me, mine, mine_came, other, other_came)


def after(x, *others):
    return lax.optimization_barrier((x, *others))[0]


def on_device(out_grad, pre_act, layer_input, weight):
    n = lax.axis_size("gx")
    rows, width = layer_input.shape
    if n != 2 * RING or rows % 16 or width % (2 * PIECES * PIECE_STEPS * 128):
        return plain(out_grad, pre_act, layer_input, weight)

    along, across = ring_pairs()
    twins = [(i, i ^ 1) for i in range(n)]

    def ring(x):
        return lax.ppermute(x, "gx", along)

    def swap(x):
        return lax.ppermute(x, "gx", twins)

    out_grad, pre_act, weight = (
        pltpu.with_memory_space_constraint(x, pltpu.HBM) for x in (out_grad, pre_act, weight)
    )
    me = lax.axis_index("gx").astype(jnp.int32).reshape(1)

    a1, twin = ring(layer_input), swap(layer_input)
    dh, dht, w = hidden(me, out_grad, pre_act, weight)
    b1 = lax.ppermute(after(layer_input, dh), "gx", across)

    def product(other, piece, w, before, *ties):
        return input_piece(me, after(dht, *ties), w, weight, before, other, piece)

    go, w = product(True, 0, w, ())
    a1 = after(a1, go[0])
    a2 = ring(a1)
    go, w = product(True, 1, w, go, a1, twin)
    b1 = after(b1, go[0])
    b2 = ring(b1)
    go, w = product(True, 2, w, go, b1)
    a2 = after(a2, go[0])
    a3, sa2 = ring(a2), swap(a2)
    go, w = product(True, 3, w, go, a2)
    b2 = after(b2, go[0])
    b3, sb2 = ring(b2), swap(b2)
    gm, w = product(False, 0, w, (), b2, sa2)
    a3 = after(a3, gm[0])
    a4, sa3 = ring(a3), swap(a3)
    own_o, behind_o, opposite_o, ahead_o = go[0], go[1:4], go[4], go[5:]
    opposite_from = swap(after(opposite_o, gm[0]))
    gm, w = product(False, 1, w, gm, a3, sb2)
    gm, w = product(False, 2, w, gm, sa3)
    sa1, sb1 = swap(a1), swap(b1)
    gm, _ = product(False, 3, w, gm, b3, opposite_from, sa1, sb1)
    own_m, behind_m, opposite_m, ahead_m = gm[0], gm[1:4], gm[4], gm[5:]
    sent = total(opposite_m, opposite_from)
    r4m = ring(sent)
    a4 = after(a4, sent)
    sa4 = swap(a4)
    from_o, from_m = [None] * 3, [None] * 3
    from_o[2], from_m[2] = swap(after(behind_m[2], sent)), swap(after(behind_o[2], sent))

    def gradient(piece, before, *ties):
        before = before[::-1]
        return weight_piece(after(dh, *ties), blocks, before, piece)

    def send(k, ahead, came, *ring_terms):
        return total(ahead[k - 1], came[k - 1], *ring_terms)

    sb3 = swap(after(b3, sent))
    blocks = (layer_input, twin, a1, b1, a2, b2, a3, b3, a4, sa4, sb1, sa1, sb2, sa2, sb3, sa3)
    gw = gradient(0, (), sent, from_o[2])
    from_o[2] = after(from_o[2], gw[1])
    sent = send(3, ahead_o, from_o)
    r3o = ring(sent)
    gw = gradient(1, gw, sent)
    sent = send(3, ahead_m, from_m, after(r4m, gw[1]))
    r3m = ring(sent)
    from_o[1], from_m[1] = swap(after(behind_m[1], sent)), swap(after(behind_o[1], sent))
    gw = gradient(2, gw, sent)
    sent = send(2, ahead_o, from_o, after(r3o, gw[1]))
    r2o = ring(sent)
    from_o[0], from_m[0] = swap(after(behind_m[0], sent)), swap(after(behind_o[0], sent))
    gw = gradient(3, gw, sent, from_m[1])
    sent = send(2, ahead_m, from_m, after(r3m, gw[1]))
    r2m = ring(sent)
    gw = gradient(4, gw, sent, from_o[0], from_m[0])
    sent = send(1, ahead_o, from_o, after(r2o, gw[1]))
    r1o = ring(sent)
    gw = gradient(5, gw, sent)
    sent = send(1, ahead_m, from_m, after(r2m, gw[1]))
    r1m = ring(sent)
    gw = gradient(6, gw, sent)
    kept_o, sent_o = halves(own_o, after(r1o, gw[1]))
    came_m = swap(sent_o)
    gw = gradient(7, gw, sent_o)
    kept_m, sent_m = halves(own_m, after(r1m, gw[0]))
    came_o = swap(sent_m)
    return (last(me, kept_m, came_m, kept_o, came_o), gw[0])


def solution(mesh):
    placed = (P("group", "gx"), P("group", "gx"), P(("group", "gx"), None), P(None, "gx"))
    return jax.shard_map(
        on_device,
        mesh=mesh,
        in_specs=placed,
        out_specs=(P(("group", "gx"), None), P(None, ("group", "gx"))),
        check_vma=False,
    )
```

```python
import math

import jax
import jax.numpy as jnp
from jax import lax
from jax.experimental import pallas as pl
from jax.experimental.pallas import tpu as pltpu
from jax.sharding import PartitionSpec as P

RING = 8
PIECE_STEPS = 2
PIECE_COST = 0.1
PIECES = 4
VMEM_LIMIT = 16 * 1024 * 1024
WHOLE = pl.BlockSpec(memory_space=pltpu.VMEM)
OUTSIDE = pl.BlockSpec(memory_space=pltpu.HBM)


def cost(microseconds):
    return pl.CostEstimate(
        flops=int(microseconds * 1.15e9), bytes_accessed=0, transcendentals=0
    )


ANYWHERE = pl.BlockSpec(memory_space=pl.ANY)
SCALAR = pl.BlockSpec(memory_space=pltpu.SMEM)


def gelu_slope(pre):
    coeff = math.sqrt(2.0 / math.pi)
    square = pre * pre
    tanh_value = jnp.tanh(pre * (coeff + coeff * 0.044715 * square))
    inner_slope = coeff + 3.0 * 0.044715 * coeff * square
    return (0.5 + 0.5 * tanh_value) * (1.0 + pre * (1.0 - tanh_value) * inner_slope)


def plain(out_grad, pre_act, layer_input, weight):
    slope = gelu_slope(pre_act.astype(jnp.float32))
    grad_hidden = (out_grad.astype(jnp.float32) * slope).astype(jnp.bfloat16)
    local_grad = lax.dot_general(
        lax.all_gather(layer_input, "gx", axis=0, tiled=True),
        grad_hidden,
        (((0,), (0,)), ((), ())),
        preferred_element_type=jnp.float32,
    )
    grad_input = lax.psum_scatter(
        lax.dot_general(
            grad_hidden, weight, (((1,), (1,)), ((), ())), preferred_element_type=jnp.float32
        ),
        "gx",
        scatter_dimension=0,
        tiled=True,
    ).astype(jnp.bfloat16)
    return (grad_input, local_grad.astype(jnp.bfloat16))


def chip_at(place):
    place = place & (RING - 1)
    return jnp.where(place < RING // 2, 2 * place, 2 * (RING - 1 - place) + 1)


def place_of(chip):
    return jnp.where(chip % 2 == 0, chip // 2, RING - 1 - chip // 2)


def ring_pairs():
    path = [2 * p if p < RING // 2 else 2 * (RING - 1 - p) + 1 for p in range(RING)]
    along, across = [], []
    for place, chip in enumerate(path):
        ahead, behind = path[(place + 1) % RING], path[(place - 1) % RING]
        along += [(2 * chip, 2 * ahead), (2 * chip + 1, 2 * behind + 1)]
        across += [(2 * chip, 2 * behind + 1), (2 * chip + 1, 2 * ahead)]
    return along, across


def chip_order(me):
    way = jnp.where(me % 2 == 0, 1, -1)
    place = place_of(me // 2)
    steps = [0, -1, -2, -3, 4, 1, 2, 3]
    return [chip_at(place + way * s + RING) for s in steps]


def hidden_kernel(me_ref, og_hbm, pre_hbm, w_hbm, dh_ref, dht_ref, w_ref, og_ref, pre_ref, sems):
    rows = dh_ref.shape[0] // (2 * RING)
    me = me_ref[0]
    copies = []
    for i, chip in enumerate(chip_order(me)):
        for j, core in enumerate((me % 2, 1 - me % 2)):
            source = pl.ds(pl.multiple_of((2 * chip + core) * rows, rows), rows)
            block = pl.ds((2 * i + j) * rows, rows)
            for k, (hbm, ref) in enumerate(((og_hbm, og_ref), (pre_hbm, pre_ref))):
                copy = pltpu.make_async_copy(
                    hbm.at[source, :], ref.at[block, :], sems.at[k, 2 * i + j]
                )
                copy.start()
                copies.append(copy)
    wide = w_ref.shape[0]
    first = first_row(me_ref, True, 0, w_hbm.shape[0] // 2, wide)
    fetch = pltpu.make_async_copy(w_hbm.at[pl.ds(first, wide), :], w_ref, sems.at[2, 0])
    for i in range(RING // 2):
        for copy in copies[8 * i : 8 * (i + 1)]:
            copy.wait()
        if i == 0:
            fetch.start()
        block = pl.ds(4 * i * rows, 4 * rows)
        pre = pre_ref[block, :].astype(jnp.float32)
        og = og_ref[block, :].astype(jnp.float32)
        dh = (og * gelu_slope(pre)).astype(jnp.bfloat16)
        dh_ref[block, :] = dh
        dht_ref[:, block] = dh.T
    fetch.wait()


def hidden(me, out_grad, pre_act, weight):
    shape, dtype = out_grad.shape, out_grad.dtype
    return pl.pallas_call(
        hidden_kernel,
        out_shape=(
            jax.ShapeDtypeStruct(shape, dtype),
            jax.ShapeDtypeStruct(shape[::-1], dtype),
            jax.ShapeDtypeStruct((weight.shape[0] // (2 * PIECES), shape[1]), dtype),
        ),
        in_specs=[SCALAR, OUTSIDE, OUTSIDE, OUTSIDE],
        out_specs=(WHOLE, WHOLE, WHOLE),
        scratch_shapes=[
            pltpu.VMEM(shape, dtype),
            pltpu.VMEM(shape, dtype),
            pltpu.SemaphoreType.DMA((3, 2 * RING)),
        ],
        compiler_params=pltpu.CompilerParams(vmem_limit_bytes=VMEM_LIMIT),
        cost_estimate=cost(1),
        name="hidden",
    )(me, out_grad, pre_act, weight)


def first_row(me_ref, other, piece, half, wide):
    core = me_ref[0] % 2
    number = 1 - core if other else core
    return pl.multiple_of(number * half + piece * wide, wide)


def input_kernel(me_ref, dht_ref, w_ref, w_hbm, *refs, other, piece, wide, more):
    outs, part_ref, sems = refs[-(RING + 2 + more) :][:RING], refs[-2], refs[-1]
    half = outs[0].shape[1]
    if more:
        following = (other, piece + 1) if piece + 1 < PIECES else (False, 0)
        fetch = pltpu.make_async_copy(
            w_hbm.at[pl.ds(first_row(me_ref, *following, half, wide), wide), :],
            refs[-3],
            sems.at[PIECE_STEPS, 0],
        )
        fetch.start()
    steps = PIECE_STEPS if other else 1
    step = wide // steps
    stores = []
    for i in range(steps):
        here = pl.ds(i * step, step)
        part = jnp.dot(w_ref[here, :], dht_ref[...], preferred_element_type=jnp.float32)
        part_ref[:, here] = part.astype(jnp.bfloat16).T
        for j, out in enumerate(outs):
            rows = out.shape[0]
            store = pltpu.make_async_copy(
                part_ref.at[pl.ds(j * rows, rows), here],
                out.at[:, pl.ds(piece * wide + i * step, step)],
                sems.at[i, j],
            )
            store.start()
            stores.append(store)
    for store in stores:
        store.wait()
    if more:
        fetch.wait()


def input_piece(me, dht, w, weight, before, other, piece):
    ff, tokens = dht.shape
    half = weight.shape[0] // 2
    wide = half // PIECES
    rows = tokens // RING
    more = other or piece + 1 < PIECES
    outs = (jax.ShapeDtypeStruct((rows, half), jnp.bfloat16),) * RING
    following = (jax.ShapeDtypeStruct((wide, ff), jnp.bfloat16),) if more else ()
    result = pl.pallas_call(
        lambda *refs: input_kernel(*refs, other=other, piece=piece, wide=wide, more=more),
        out_shape=outs + following,
        in_specs=[SCALAR, WHOLE, WHOLE, OUTSIDE] + [ANYWHERE] * len(before),
        out_specs=(ANYWHERE,) * RING + (WHOLE,) * len(following),
        input_output_aliases={4 + i: i for i in range(len(before))},
        scratch_shapes=[
            pltpu.VMEM((tokens, wide), jnp.bfloat16),
            pltpu.SemaphoreType.DMA((PIECE_STEPS + 1, RING)),
        ],
        compiler_params=pltpu.CompilerParams(vmem_limit_bytes=VMEM_LIMIT),
        cost_estimate=cost(PIECE_COST),
        name="input_piece",
    )(me, dht, w, weight, *before)
    return result[:RING], (result[RING] if more else None)


def weight_kernel(dh_ref, *refs, piece, wide, step):
    blocks, refs = refs[: 2 * RING], refs[2 * RING :]
    out_hbm, stage, sems = refs[-3:]
    width, columns = out_hbm.shape
    copies = []

    def store(source, number, i):
        here = pl.ds(i * step, step)
        rows = pl.ds(number * wide, wide)
        copy = pltpu.make_async_copy(
            source.at[:, here], out_hbm.at[rows, here], sems.at[piece - number, i]
        )
        copy.start()
        copies.append(copy)

    if piece:
        for i in range(columns // step):
            store(refs[0], piece - 1, i)
    x = jnp.concatenate([b[:, pl.ds(piece * wide, wide)] for b in blocks], axis=0).T
    for i in range(columns // step):
        here = pl.ds(i * step, step)
        stage[:, here] = jnp.dot(
            x, dh_ref[:, here], preferred_element_type=jnp.float32
        ).astype(jnp.bfloat16)
        if (piece + 1) * wide == width:
            store(stage, piece, i)
    for copy in copies:
        copy.wait()


def weight_piece(dh, blocks, before, piece):
    tokens, ff = dh.shape
    width = blocks[0].shape[1]
    wide = width // (2 * PIECES)
    step = 512 if ff % 512 == 0 else 128
    ends = piece == 2 * PIECES - 1
    stage = jax.ShapeDtypeStruct((wide, ff), jnp.bfloat16)
    return pl.pallas_call(
        lambda *refs: weight_kernel(*refs, piece=piece, wide=wide, step=step),
        out_shape=(jax.ShapeDtypeStruct((width, ff), jnp.bfloat16),) + (stage,) * (not ends),
        in_specs=[WHOLE] * (1 + 2 * RING) + ([WHOLE, OUTSIDE] if before else []),
        out_specs=(OUTSIDE,) + (WHOLE,) * (not ends),
        input_output_aliases={2 + 2 * RING: 0} if before else {},
        scratch_shapes=[pltpu.VMEM(stage.shape, stage.dtype)] * ends
        + [pltpu.SemaphoreType.DMA((2, ff // step))],
        compiler_params=pltpu.CompilerParams(vmem_limit_bytes=VMEM_LIMIT),
        cost_estimate=cost(PIECE_COST),
        name="weight_piece",
    )(dh, *blocks, *before)


def total_kernel(part_ref, twin_ref, *refs):
    rows = part_ref.shape[0] // 2
    for here, there in ((pl.ds(0, rows), pl.ds(rows, rows)), (pl.ds(rows, rows), pl.ds(0, rows))):
        total = part_ref[here, :].astype(jnp.float32) + twin_ref[there, :].astype(jnp.float32)
        for ref in refs[:-1]:
            total = total + ref[here, :].astype(jnp.float32)
        refs[-1][here, :] = total.astype(refs[-1].dtype)


def total(*terms):
    return pl.pallas_call(
        total_kernel,
        out_shape=jax.ShapeDtypeStruct(terms[0].shape, terms[0].dtype),
        in_specs=[WHOLE] * len(terms),
        out_specs=WHOLE,
        compiler_params=pltpu.CompilerParams(vmem_limit_bytes=VMEM_LIMIT),
        cost_estimate=cost(0.1),
        name="total",
    )(*terms)


def halves_kernel(own_ref, came_ref, kept_ref, sent_ref):
    rows = kept_ref.shape[0]
    for ref, here in ((kept_ref, pl.ds(0, rows)), (sent_ref, pl.ds(rows, rows))):
        both = own_ref[here, :].astype(jnp.float32) + came_ref[here, :].astype(jnp.float32)
        ref[...] = both.astype(ref.dtype)


def halves(own, came):
    shape = (own.shape[0] // 2, own.shape[1])
    return pl.pallas_call(
        halves_kernel,
        out_shape=(
            jax.ShapeDtypeStruct(shape, jnp.float32),
            jax.ShapeDtypeStruct(shape, jnp.bfloat16),
        ),
        in_specs=[WHOLE, WHOLE],
        out_specs=(WHOLE, WHOLE),
        compiler_params=pltpu.CompilerParams(vmem_limit_bytes=VMEM_LIMIT),
        cost_estimate=cost(0.1),
        name="halves",
    )(own, came)


def last_kernel(me_ref, mine_ref, mine_came_ref, other_ref, other_came_ref, out_ref):
    core = me_ref[0] % 2
    half = mine_ref.shape[1]
    pairs = ((core, mine_ref, mine_came_ref), (1 - core, other_ref, other_came_ref))
    for number, kept, came in pairs:
        here = pl.ds(pl.multiple_of(number * half, half), half)
        out_ref[:, here] = (kept[...] + came[...].astype(jnp.float32)).astype(out_ref.dtype)


def last(me, mine, mine_came, other, other_came):
    shape = (mine.shape[0], 2 * mine.shape[1])
    return pl.pallas_call(
        last_kernel,
        out_shape=jax.ShapeDtypeStruct(shape, jnp.bfloat16),
        in_specs=[SCALAR] + [WHOLE] * 4,
        out_specs=WHOLE,
        compiler_params=pltpu.CompilerParams(vmem_limit_bytes=VMEM_LIMIT),
        cost_estimate=cost(0.3),
        name="last",
    )(me, mine, mine_came, other, other_came)


def after(x, *others):
    return lax.optimization_barrier((x, *others))[0]


def on_device(out_grad, pre_act, layer_input, weight):
    n = lax.axis_size("gx")
    rows, width = layer_input.shape
    if n != 2 * RING or rows % 16 or width % (2 * PIECES * PIECE_STEPS * 128):
        return plain(out_grad, pre_act, layer_input, weight)

    along, across = ring_pairs()
    twins = [(i, i ^ 1) for i in range(n)]

    def ring(x):
        return lax.ppermute(x, "gx", along)

    def swap(x):
        return lax.ppermute(x, "gx", twins)

    out_grad, pre_act, weight = (
        pltpu.with_memory_space_constraint(x, pltpu.HBM) for x in (out_grad, pre_act, weight)
    )
    me = lax.axis_index("gx").astype(jnp.int32).reshape(1)

    a1, twin = ring(layer_input), swap(layer_input)
    dh, dht, w = hidden(me, out_grad, pre_act, weight)
    b1 = lax.ppermute(after(layer_input, dh), "gx", across)

    def product(other, piece, w, before, *ties):
        return input_piece(me, after(dht, *ties), w, weight, before, other, piece)

    go, w = product(True, 0, w, ())
    a1 = after(a1, go[0])
    a2, sa1 = ring(a1), swap(a1)
    go, w = product(True, 1, w, go, a1, twin)
    b1 = after(b1, go[0])
    b2, sb1 = ring(b1), swap(b1)
    go, w = product(True, 2, w, go, b1, sa1)
    a2 = after(a2, go[0])
    a3, sa2 = ring(a2), swap(a2)
    go, w = product(True, 3, w, go, a2, sb1)
    b2 = after(b2, go[0])
    b3, sb2 = ring(b2), swap(b2)
    gm, w = product(False, 0, w, (), b2, sa2)
    a3 = after(a3, gm[0])
    a4, sa3 = ring(a3), swap(a3)
    own_o, behind_o, opposite_o, ahead_o = go[0], go[1:4], go[4], go[5:]
    opposite_from = swap(after(opposite_o, gm[0]))
    gm, w = product(False, 1, w, gm, a3, sb2)
    gm, w = product(False, 2, w, gm, sa3)
    gm, _ = product(False, 3, w, gm, b3, opposite_from)
    own_m, behind_m, opposite_m, ahead_m = gm[0], gm[1:4], gm[4], gm[5:]
    sent = total(opposite_m, opposite_from)
    r4m = ring(sent)
    a4 = after(a4, sent)
    sa4 = swap(a4)
    from_o, from_m = [None] * 3, [None] * 3
    from_o[2], from_m[2] = swap(after(behind_m[2], sent)), swap(after(behind_o[2], sent))

    def gradient(piece, before, *ties):
        before = before[::-1]
        return weight_piece(after(dh, *ties), blocks, before, piece)

    def send(k, ahead, came, *ring_terms):
        return total(ahead[k - 1], came[k - 1], *ring_terms)

    sb3 = swap(after(b3, sent))
    blocks = (layer_input, twin, a1, b1, a2, b2, a3, b3, a4, sa4, sb1, sa1, sb2, sa2, sb3, sa3)
    gw = gradient(0, (), sent, from_o[2])
    from_o[2] = after(from_o[2], gw[1])
    sent = send(3, ahead_o, from_o)
    r3o = ring(sent)
    gw = gradient(1, gw, sent)
    sent = send(3, ahead_m, from_m, after(r4m, gw[1]))
    r3m = ring(sent)
    from_o[1], from_m[1] = swap(after(behind_m[1], sent)), swap(after(behind_o[1], sent))
    gw = gradient(2, gw, sent)
    sent = send(2, ahead_o, from_o, after(r3o, gw[1]))
    r2o = ring(sent)
    from_o[0], from_m[0] = swap(after(behind_m[0], sent)), swap(after(behind_o[0], sent))
    gw = gradient(3, gw, sent, from_m[1])
    sent = send(2, ahead_m, from_m, after(r3m, gw[1]))
    r2m = ring(sent)
    gw = gradient(4, gw, sent, from_o[0], from_m[0])
    sent = send(1, ahead_o, from_o, after(r2o, gw[1]))
    r1o = ring(sent)
    gw = gradient(5, gw, sent)
    sent = send(1, ahead_m, from_m, after(r2m, gw[1]))
    r1m = ring(sent)
    gw = gradient(6, gw, sent)
    kept_o, sent_o = halves(own_o, after(r1o, gw[1]))
    came_m = swap(sent_o)
    gw = gradient(7, gw, sent_o)
    kept_m, sent_m = halves(own_m, after(r1m, gw[0]))
    came_o = swap(sent_m)
    return (last(me, kept_m, came_m, kept_o, came_o), gw[0])


def solution(mesh):
    placed = (P("group", "gx"), P("group", "gx"), P(("group", "gx"), None), P(None, "gx"))
    return jax.shard_map(
        on_device,
        mesh=mesh,
        in_specs=placed,
        out_specs=(P(("group", "gx"), None), P(None, ("group", "gx"))),
        check_vma=False,
    )
```
